256 devices in a mesh: seq: 16 (over x, y), exp: 16 (over z, core).
Axes of the slice: x: 4, y: 4, z: 8, core: 2. Of those that a mesh axis runs over, the one named last changes fastest.
Arguments:
- queries: bfloat16 [8192, 4096], P('seq', 'exp'), may hold values from -6 to 6
- keys: bfloat16 [8192, 4096], P('seq', 'exp'), may hold values from -6 to 6
- values: bfloat16 [8192, 4096], P('seq', 'exp'), may hold values from -6 to 6
- log_decay: float32 [8192, 32], P('seq', 'exp'), may hold values from -1.52 to 0
- residual: bfloat16 [8192, 3072], P(('seq', 'exp')), may hold values from -6 to 6
- out_weight: bfloat16 [4096, 3072], P('exp'), may hold values from -0.09375 to 0.09375
- router: bfloat16 [3072, 16], replicated, may hold values from -0.109375 to 0.109375
- w_gate: bfloat16 [16, 3072, 6144], P('exp', None, 'seq'), may hold values from -0.109375 to 0.109375
- w_up: bfloat16 [16, 3072, 6144], P('exp', None, 'seq'), may hold values from -0.109375 to 0.109375
- w_down: bfloat16 [16, 6144, 3072], P('exp', 'seq'), may hold values from -0.078125 to 0.078125
- routes: int32 [8192, 2], P(('seq', 'exp')), may hold values from 0 to 15, all different within a row; in each aligned block of 32 rows (0 to 31, 32 to 63, ...) at most 6 rows name the same one
Outputs:
- output: bfloat16 [8192, 3072], P(('seq', 'exp'))
The draws below stay inside these ranges and needn't reach their ends.
Inputs may be any that keep to these rules, and one draw needn't show every extreme that they name: `routes`: no expert is named by more than 6 of the rows of one device (aligned blocks of 32 rows); a row names 2 different experts.
All inputs are finite; a program needn't handle non-finite values.
Results may differ from the reference program's by a relative error of at most 0.022.
Values may be sent and summed in bfloat16 or wider, within the bound.
No kernel may reach another device: no remote copies, remote signals or barrier semaphores. Data moves between devices by JAX's collectives and lax.ppermute only.
A program may use at most 128 MiB of HBM per device.

```python
import math
import jax
import jax.numpy as jnp
import numpy as np
from jax import lax

D = 3072
HEAD_DIM = 128
HEAD_DEV = 2
FF = 6144
TOP = 2
TOK_DEV = 32
HEAD_COUNT = 32
T_SEQ = 512
TOKEN_COUNT = 8192
EXPERTS = 16
BLOCK = 512
CAP = 6
N_SEQ = 16
N_EXP = 16
DEVICES = 256


def draw_log_decay(key, part):
    parallel_lanes = jax.random.split(key, 6)
    rapid_share = 0.5
    rapid_heads = jax.random.uniform(parallel_lanes[0], (HEAD_COUNT,), jnp.float32) < rapid_share
    rapid_rate = jax.random.uniform(parallel_lanes[1], (HEAD_COUNT,), jnp.float32, minval=1.0 / 50.0, maxval=1.0 / 30.0)
    baseline_decay_rate = jnp.where(rapid_heads, rapid_rate, 0.5 / TOKEN_COUNT)
    sequence_segment = jnp.exp(jax.random.uniform(parallel_lanes[2], (TOKEN_COUNT // T_SEQ, HEAD_COUNT), jnp.float32, minval=-0.7, maxval=0.7))
    sequence_segment = jnp.repeat(sequence_segment, T_SEQ, axis=0)
    jitter_level = jnp.exp(jax.random.uniform(parallel_lanes[3], (TOKEN_COUNT, HEAD_COUNT), jnp.float32, minval=-0.7, maxval=0.7))
    spike_location = jax.random.randint(parallel_lanes[4], (2, HEAD_COUNT), 0, TOKEN_COUNT)
    spike_magnitude = jax.random.uniform(parallel_lanes[5], (2, HEAD_COUNT), jnp.float32, minval=0.22, maxval=0.69)
    token_positions = jnp.arange(TOKEN_COUNT)[:, None]
    sudden_spike = jnp.where(token_positions == spike_location[0][None, :], spike_magnitude[0][None, :], 0.0)
    sudden_spike = sudden_spike + jnp.where(token_positions == spike_location[1][None, :], spike_magnitude[1][None, :], 0.0)
    return -(baseline_decay_rate[None, :] * sequence_segment * jitter_level + sudden_spike)


def block_levels(rng, shape, cuts, least, top_value):
    loudness = 1.0
    for axis_at, shards_of in cuts:
        steps = jax.random.uniform(jax.random.fold_in(jax.random.fold_in(rng, 6), axis_at), (shards_of,), jnp.float32, least / len(cuts), top_value / len(cuts))
        loudness = loudness * jnp.repeat(jnp.exp(steps), shape[axis_at] // shards_of).reshape((-1,) + (1,) * (len(shape) - 1 - axis_at))
    return loudness


def deal_out(rng, own, number, rows, number_of, top, reach, lean):
    order = jax.random.permutation(rng, number_of)
    packed, ordinary = load_shares(number_of, rows * top, reach, lean, True), load_shares(number_of, rows * top, reach, lean, False)
    places = jnp.arange(number_of)

    def named(lengths, offset_by):
        used = int((lengths > 0).sum())
        fixed = max(1, used // 4)
        moved = fixed + (places - fixed + offset_by * (used - fixed)) % max(1, number_of - fixed)
        return jnp.zeros((number_of,), jnp.int32).at[order[jnp.where(places < fixed, places, moved)]].set(jnp.asarray(lengths, jnp.int32))

    lengths = jnp.where(number % 4 == 0, named(packed, number // 4), named(ordinary, number - number // 4 - 1))
    mixed = jax.random.permutation(jax.random.fold_in(own, 3), number_of)
    giver, receiver = mixed[0:number_of // 2 * 2:2], mixed[1:number_of // 2 * 2:2]
    margin = jnp.minimum(lengths[giver] - 1, reach - lengths[receiver]) // 2
    margin = jnp.where((giver == order[0]) | (receiver == order[0]) | (lengths[receiver] == 0), 0, jnp.maximum(margin, 0))
    moved = jax.random.randint(jax.random.fold_in(own, 4), (number_of // 2,), 0, 1 << 20) % (margin + 1)
    lengths = lengths.at[giver].add(-moved).at[receiver].add(moved)
    items = jnp.searchsorted(jnp.cumsum(lengths), jnp.arange(rows * top), side="right").astype(jnp.int32)
    table = items.reshape(top, rows).T
    table = table[jax.random.permutation(jax.random.fold_in(own, 1), rows)]
    offset_by = jax.random.randint(jax.random.fold_in(own, 2), (rows, 1), 0, top)
    return jnp.take_along_axis(table, (jnp.arange(top)[None, :] + offset_by) % top, axis=1)


def load_shares(number_of, total, reach, skew, full):
    weights = [(1 << 20) // math.isqrt(rank ** skew) + 1 for rank in range(1, number_of + 1)]
    largest = reach if full else min(reach, max(-(-total // number_of), total * weights[0] // sum(weights)))
    least = 1 if total - largest >= number_of - 1 else 0
    counts, rest = [largest] + [least] * (number_of - 1), total - largest - least * (number_of - 1)
    while rest > 0:
        movable = [i for i in range(1, number_of) if counts[i] < largest] or [i for i in range(1, number_of) if counts[i] < reach]
        whole, budget = sum([weights[i] for i in movable]), rest
        for i in movable:
            extra = min(reach - counts[i], max(1, budget * weights[i] // whole), rest)
            counts[i] = counts[i] + extra
            rest = rest - extra
    return np.array(counts)


def bell_draw(rng, extent, scale, bound, shards=(), kind=jnp.bfloat16):
    result = jax.random.normal(rng, extent, jnp.float32) * scale
    if len(shards) > 0:
        result = block_levels(rng, extent, shards, -0.22, 0.18) * result
    return jnp.clip(result, min=-bound, max=bound).astype(kind)


def setup_inputs(seed: int = 0) -> dict:
    streams_of = jax.random.split(jax.random.key(seed), 12)
    queries = bell_draw(streams_of[0], (TOKEN_COUNT, HEAD_COUNT * HEAD_DIM), 1.0, 6.0, ((0, 16), (1, 16)))
    keys = bell_draw(streams_of[1], (TOKEN_COUNT, HEAD_COUNT * HEAD_DIM), 1.0, 6.0, ((0, 16), (1, 16)))
    values = bell_draw(streams_of[2], (TOKEN_COUNT, HEAD_COUNT * HEAD_DIM), 1.0, 6.0, ((0, 16), (1, 16)))
    log_decay = draw_log_decay(jax.random.fold_in(streams_of[11], 71), 0)
    residual = bell_draw(streams_of[4], (TOKEN_COUNT, D), 1.0, 6.0, ((0, 256),))
    out_weight = bell_draw(streams_of[5], (HEAD_COUNT * HEAD_DIM, D), (HEAD_COUNT * HEAD_DIM) ** -0.5, 0.09375, ((0, 16),))
    router = bell_draw(streams_of[6], (D, EXPERTS), D ** -0.5, 0.109375)
    w_gate = bell_draw(streams_of[7], (EXPERTS, D, FF), D ** -0.5, 0.109375, ((0, 16), (2, 16)))
    w_up = bell_draw(streams_of[8], (EXPERTS, D, FF), D ** -0.5, 0.109375, ((0, 16), (2, 16)))
    w_down = bell_draw(streams_of[9], (EXPERTS, FF, D), FF ** -0.5, 0.078125, ((0, 16), (1, 16)))
    routes_keys = jax.random.split(jax.random.fold_in(streams_of[10], 1), TOKEN_COUNT // TOK_DEV)
    routes_turns = jax.random.permutation(jax.random.fold_in(streams_of[10], 3), TOKEN_COUNT // TOK_DEV)
    routes = jax.vmap(lambda own, number: deal_out(jax.random.fold_in(streams_of[10], 2), own, number, TOK_DEV, EXPERTS, TOP, CAP, 1))(routes_keys, routes_turns).reshape((TOKEN_COUNT, TOP))
    return {"queries": queries, "keys": keys, "values": values, "log_decay": log_decay, "residual": residual, "out_weight": out_weight, "router": router, "w_gate": w_gate, "w_up": w_up, "w_down": w_down, "routes": routes}


HIGHEST = lax.Precision.HIGHEST

def into_blocks(array, block_rows):
    return array.reshape((array.shape[0] // block_rows, block_rows) + array.shape[1:])

def sweep_outputs(query_heads, key_heads, value_heads, decays, start_state, block_rows):

    def one_block(state_mat, inputs):
        query_block, key_block, value_block, decay_block = inputs
        cumulative = jnp.cumsum(decay_block, axis=0)
        rows_count = decay_block.shape[0]
        causal = jnp.arange(rows_count)[:, None] >= jnp.arange(rows_count)[None, :]
        differences = cumulative[:, None, :] - cumulative[None, :, :]
        damping = jnp.where(causal[:, :, None], jnp.exp(jnp.minimum(differences, 0.0)), 0.0)
        query_float = query_block.astype(jnp.float32)
        key_float = key_block.astype(jnp.float32)
        value_float = value_block.astype(jnp.float32)
        scores = jnp.einsum('ihd,jhd->ijh', query_float, key_float, precision=HIGHEST)
        within = jnp.einsum('ijh,jhd->ihd', scores * damping, value_float, precision=HIGHEST)
        scaled_query = query_float * jnp.exp(cumulative)[:, :, None]
        carried_part = jnp.einsum('ihd,hde->ihe', scaled_query, state_mat, precision=HIGHEST)
        tail_sum = cumulative[-1]
        scaled_key = key_float * jnp.exp(tail_sum[None, :] - cumulative)[:, :, None]
        new_state = jnp.exp(tail_sum)[:, None, None] * state_mat + jnp.einsum('jhd,jhe->hde', scaled_key, value_float, precision=HIGHEST)
        return (new_state, within + carried_part)
    final_state, outputs = lax.scan(one_block, start_state, (into_blocks(query_heads, block_rows), into_blocks(key_heads, block_rows), into_blocks(value_heads, block_rows), into_blocks(decays, block_rows)))
    return (outputs.reshape(query_heads.shape), final_state)

def reference(queries, keys, values, log_decay, residual, out_weight, router, w_gate, w_up, w_down, routes):
    query_heads = queries.reshape(TOKEN_COUNT, HEAD_COUNT, HEAD_DIM)
    key_heads = keys.reshape(TOKEN_COUNT, HEAD_COUNT, HEAD_DIM)
    value_heads = values.reshape(TOKEN_COUNT, HEAD_COUNT, HEAD_DIM)
    start_state = jnp.zeros((HEAD_COUNT, HEAD_DIM, HEAD_DIM), jnp.float32)
    mixed, unused = sweep_outputs(query_heads, key_heads, value_heads, log_decay, start_state, BLOCK)
    scale_back = lax.rsqrt(lax.optimization_barrier(jnp.mean(mixed * mixed, axis=-1, keepdims=True)) + 1e-06)
    heads_out = (mixed * scale_back).astype(jnp.bfloat16).reshape(TOKEN_COUNT, HEAD_COUNT * HEAD_DIM)
    group_cols = HEAD_DEV * HEAD_DIM

    def add_group(index, total):
        offset = (index * group_cols).astype(jnp.int32)
        columns = lax.dynamic_slice_in_dim(heads_out, offset, group_cols, 1)
        weight_rows = lax.dynamic_slice_in_dim(out_weight, offset, group_cols, 0)
        partial_sum = jnp.dot(columns, weight_rows, preferred_element_type=jnp.float32).astype(jnp.bfloat16)
        partial_sum = lax.optimization_barrier(partial_sum)
        return total + partial_sum.astype(jnp.float32)
    attn = lax.fori_loop(0, N_EXP, add_group, jnp.zeros((TOKEN_COUNT, D), jnp.float32))
    hidden = residual.astype(jnp.float32) + attn
    normed = (hidden * lax.rsqrt(lax.optimization_barrier(jnp.mean(hidden * hidden, axis=-1, keepdims=True)) + 1e-06)).astype(jnp.bfloat16)
    logits = jnp.dot(normed, router, preferred_element_type=jnp.float32)
    picked = jnp.take_along_axis(jax.nn.sigmoid(logits), routes, axis=1)
    gates = picked / lax.optimization_barrier(jnp.sum(picked, axis=1, keepdims=True))
    device_routes = routes.reshape(DEVICES, TOK_DEV * TOP)
    onehot = (device_routes[:, :, None] == jnp.arange(EXPERTS, dtype=jnp.int32)[None, None, :]).astype(jnp.int32)
    running = jnp.cumsum(onehot, axis=1)
    slot = lax.optimization_barrier(jnp.sum(onehot * running, axis=2)) - 1
    device_ids = jnp.arange(DEVICES, dtype=jnp.int32)[:, None]
    row_ids = (device_ids * CAP + slot).reshape(-1).astype(jnp.int32)
    expert_ids = device_routes.reshape(-1).astype(jnp.int32)
    copies = jnp.repeat(normed, TOP, axis=0)
    buffers = jnp.zeros((EXPERTS, DEVICES * CAP, D), jnp.bfloat16).at[expert_ids, row_ids].set(copies)
    units = FF // N_SEQ

    def one_expert(operands):
        token_rows, gate_mat, up_mat, down_mat = operands
        gate_part = jnp.dot(token_rows, gate_mat, preferred_element_type=jnp.float32)
        up_part = jnp.dot(token_rows, up_mat, preferred_element_type=jnp.float32)
        expert_hidden = (jax.nn.silu(gate_part) * up_part).astype(jnp.bfloat16)
        pieces = jnp.einsum('rgf,gfd->grd', expert_hidden.reshape(-1, N_SEQ, units).astype(jnp.float32), down_mat.reshape(N_SEQ, units, D).astype(jnp.float32), precision=HIGHEST)
        pieces = lax.optimization_barrier(pieces.astype(jnp.bfloat16))
        return lax.optimization_barrier(jnp.sum(pieces.astype(jnp.float32), axis=0)).astype(jnp.bfloat16)
    results = lax.map(one_expert, (buffers, w_gate, w_up, w_down))
    picked_rows = results[expert_ids, row_ids].astype(jnp.float32).reshape(TOKEN_COUNT, TOP, D)
    return (hidden + lax.optimization_barrier(jnp.sum(gates[:, :, None] * picked_rows, axis=1))).astype(jnp.bfloat16)
```

```python
import jax
import jax.numpy as jnp
from jax import lax
from jax.sharding import Mesh, PartitionSpec as P

D = 3072
HEAD_DIM = 128
TOK = 32
CAP = 6
QUARTERS = 4
QCOLS = D // QUARTERS
NX, NY, NZ, NC = 4, 4, 8, 2
SIZES = {"x": NX, "y": NY, "z": NZ, "c": NC}
NEAR, FAR = (0, 1, 7, 2), (6, 3, 5, 4)
HIGHEST = lax.Precision.HIGHEST
F32, BF16 = jnp.float32, jnp.bfloat16


def shift(v, axis, by):
    n = SIZES[axis]
    return lax.ppermute(v, axis, [(i, (i + by) % n) for i in range(n)])


def ahead(v, axis):
    return [v, shift(v, axis, -1), shift(v, axis, 2), shift(v, axis, 1)]


def ahead_split(v, axis):
    up, down = shift(v, axis, -1), shift(v, axis, 1)
    half = v.shape[0] // 2
    far = jnp.concatenate([shift(up[:half], axis, -1), shift(down[half:], axis, 1)], axis=0)
    return [v, up, far, down]


def dot(a, b):
    return jnp.dot(a, b, preferred_element_type=F32)


def split_hi_lo(v):
    hi = v.astype(BF16)
    return hi, (v - hi.astype(F32)).astype(BF16)


def pack(state, total):
    hi, lo = split_hi_lo(total)
    rows = jnp.stack([hi, lo], axis=1)[:, :, None]
    rows = jnp.broadcast_to(rows, (2, 2, HEAD_DIM))
    rows = jnp.concatenate([rows, jnp.zeros((2, 6, HEAD_DIM), BF16)], axis=1)
    return jnp.concatenate([state.astype(BF16), rows], axis=1)


def unpack(message):
    m = message.astype(F32)
    return m[:, :HEAD_DIM], m[:, HEAD_DIM, 0] + m[:, HEAD_DIM + 1, 0]


def fold(messages, own, place):
    states, totals = zip(own, *[unpack(m) for m in messages])
    where = [(place + SIZES["x"] - d) % 4 for d in range(4)]
    ordered = [sum(jnp.where(where[d] == j, totals[d], 0.0) for d in range(4)) for j in range(4)]
    before = jnp.zeros_like(states[0])
    everything = jnp.zeros_like(states[0])
    for d in range(4):
        till_here = sum(
            jnp.where((j > where[d]) & (j < place), ordered[j], 0.0) for j in range(4)
        )
        till_end = sum(jnp.where(j > where[d], ordered[j], 0.0) for j in range(4))
        weight = jnp.where(where[d] < place, jnp.exp(till_here), 0.0)
        before = before + weight[:, None, None] * states[d]
        everything = everything + jnp.exp(till_end)[:, None, None] * states[d]
    total_before = sum(jnp.where(j < place, ordered[j], 0.0) for j in range(4))
    return before, total_before, everything, sum(ordered)


def incoming(state, total):
    message = pack(state, total)
    row = [shift(message, "y", d) for d in (1, 2, 3)]
    before, total_before, everything, total_row = fold(
        row, (state, total), lax.axis_index("y")
    )
    message = pack(everything, total_row)
    rows = [shift(message, "x", d) for d in (1, 2, 3)]
    earlier, _, _, _ = fold(rows, (everything, total_row), lax.axis_index("x"))
    return before + jnp.exp(total_before)[:, None, None] * earlier


def attention(queries, keys, values, log_decay):
    rows = queries.shape[0]
    q = queries.reshape(rows, 2, HEAD_DIM)
    k = keys.reshape(rows, 2, HEAD_DIM)
    v = values.reshape(rows, 2, HEAD_DIM)
    cumulative = jnp.cumsum(log_decay, axis=0)
    tail = cumulative[-1]
    scaled_key = k.astype(F32) * jnp.exp(tail[None, :] - cumulative)[:, :, None]
    value_float = v.astype(F32)
    state = jnp.einsum("jhd,jhe->hde", scaled_key, value_float, precision=HIGHEST)
    state_in = incoming(state, tail)
    causal = jnp.arange(rows)[:, None] >= jnp.arange(rows)[None, :]
    differences = cumulative[:, None, :] - cumulative[None, :, :]
    damping = jnp.where(causal[:, :, None], jnp.exp(jnp.minimum(differences, 0.0)), 0.0)
    scores = jnp.einsum("ihd,jhd->ijh", q, k, preferred_element_type=F32)
    within = jnp.einsum("ijh,jhd->ihd", scores * damping, value_float, precision=HIGHEST)
    scaled_query = q.astype(F32) * jnp.exp(cumulative)[:, :, None]
    mixed = within + jnp.einsum("ihd,hde->ihe", scaled_query, state_in, precision=HIGHEST)
    scale = lax.rsqrt(jnp.mean(mixed * mixed, axis=-1, keepdims=True) + 1e-06)
    return (mixed * scale).astype(BF16).reshape(rows, 2 * HEAD_DIM)


def unfold_matrix():
    row = jnp.arange(48)
    place, core, slot = row // 12, (row // 6) % 2, row % 6
    quarter = jnp.arange(QUARTERS)[:, None]
    source = place * 48 + core * 24 + quarter * 6 + slot
    return (source[:, :, None] == jnp.arange(192)[None, None, :]).astype(BF16)


def shards(
    queries, keys, values, log_decay, residual, out_weight, router, w_gate, w_up, w_down, routes
):
    z, c = lax.axis_index("z"), lax.axis_index("c")
    x, y = lax.axis_index("x"), lax.axis_index("y")
    half_cols = D // 2
    down_x = lax.all_gather(w_down[0][:, :half_cols], "x", axis=0)
    down_y = lax.all_gather(w_down[0][:, half_cols:], "y", axis=0)
    weight_pair = jnp.concatenate([out_weight, shift(out_weight, "c", 1)], axis=0)
    gate_up = jnp.concatenate([w_gate[0], w_up[0]], axis=1)

    ids = jnp.arange(16)
    relative = 2 * ((z + ids % NZ) % NZ) + (c ^ (ids // NZ))
    named = (routes[:, :, None] == relative[None, None, :]).any(axis=1)
    member = named.astype(F32)
    earlier = (jnp.arange(TOK)[:, None] > jnp.arange(TOK)[None, :]).astype(F32)
    slot = jnp.dot(earlier, member).astype(jnp.int32)
    router_rel = dot(
        router, (ids[:, None] == relative[None, :]).astype(BF16)
    ).astype(BF16)
    chosen = named[:, :, None] & (slot[:, :, None] == jnp.arange(CAP)[None, None, :])
    chosen = chosen.reshape(TOK, NC, NZ, CAP).transpose(1, 2, 3, 0)
    same = jnp.eye(QUARTERS, dtype=jnp.bool_)
    dispatch = chosen[:, :, None, :, None, :] & same[None, None, :, None, :, None]
    dispatch = dispatch.reshape(NC, NZ * QUARTERS * CAP, QUARTERS * TOK)
    dispatch_bf = dispatch.astype(BF16)

    heads_out = attention(queries, keys, values, log_decay).reshape(NZ, NC, TOK, 2 * HEAD_DIM)
    mine = jnp.where(c == 0, heads_out[:, 0], heads_out[:, 1]).reshape(NZ * TOK, 2 * HEAD_DIM)
    theirs = jnp.where(c == 0, heads_out[:, 1], heads_out[:, 0]).reshape(NZ * TOK, 2 * HEAD_DIM)
    both = jnp.concatenate([mine, shift(theirs, "c", 1)], axis=1)
    projected = dot(both, weight_pair).astype(BF16).reshape(NZ, TOK, D)
    attn = lax.dynamic_index_in_dim(projected, z, 0, keepdims=False).astype(F32)
    parts = [
        shift(lax.dynamic_index_in_dim(projected, (z + d) % NZ, 0, keepdims=False), "z", d)
        for d in (4, 3, 5, 2, 6, 1, 7)
    ]
    for part in parts:
        attn = attn + part.astype(F32)
    hidden = residual.astype(F32) + attn
    normed = (hidden * lax.rsqrt(jnp.mean(hidden * hidden, axis=-1, keepdims=True) + 1e-06)).astype(
        BF16
    )
    logits = dot(normed, router_rel)
    picked = jax.nn.sigmoid(logits) * member
    gates = picked / jnp.sum(picked, axis=1, keepdims=True)

    folded = jnp.concatenate(
        [normed[:, i * QCOLS : (i + 1) * QCOLS] for i in range(QUARTERS)], axis=0
    )
    keep = dot(dispatch_bf[0], folded).astype(BF16).reshape(NZ, 24, QCOLS)
    give = shift(dot(dispatch_bf[1], folded).astype(BF16), "c", 1).reshape(NZ, 24, QCOLS)
    leaving = jnp.concatenate([keep, give], axis=1)
    arrived = {d: (shift(leaving[d], "z", d) if d else leaving[0]) for d in NEAR + FAR}
    unfold = unfold_matrix()

    def unfolded(places):
        block = jnp.concatenate([arrived[d] for d in places], axis=0)
        return jnp.concatenate(
            [dot(unfold[i], block).astype(BF16) for i in range(QUARTERS)], axis=1
        )

    first, second = unfolded(NEAR), unfolded(FAR)
    by_y = ahead_split(jnp.concatenate(ahead(first, "x"), axis=0), "y")
    by_x = ahead_split(jnp.concatenate(ahead(second, "y"), axis=0), "x")

    def expert_hidden(blocks):
        product = dot(jnp.concatenate(blocks, axis=0), gate_up)
        gate_part, up_part = jnp.split(product, 2, axis=1)
        out = (jax.nn.silu(gate_part) * up_part).astype(BF16)
        return [o.reshape(4, 48, -1) for o in jnp.split(out, len(blocks), axis=0)]

    h1, h2 = [None] * 4, [None] * 4
    h1[0], h2[0] = expert_hidden([by_y[0], by_x[0]])
    h1[1], h1[3], h2[1], h2[3] = expert_hidden([by_y[1], by_y[3], by_x[1], by_x[3]])
    h1[2], h2[2] = expert_hidden([by_y[2], by_x[2]])

    def send_x(dx):
        return jnp.stack([t for dy in range(4) for t in (h1[dy][dx], h2[dx][dy])]).reshape(384, -1)

    def send_y(dy):
        return jnp.stack([t for dx in range(4) for t in (h1[dy][dx], h2[dx][dy])]).reshape(384, -1)

    hid_x = [send_x(0)] + [shift(send_x(d), "x", d) for d in (1, 2, 3)]
    hid_y = [send_y(0)] + [shift(send_y(d), "y", d) for d in (1, 2, 3)]

    def down(pieces, weights, place):
        total = 0.0
        for d in range(4):
            slice_of = lax.dynamic_index_in_dim(weights, (place - d) % 4, 0, keepdims=False)
            total = total + dot(pieces[d], slice_of)
        return total.astype(BF16).reshape(4, 96, half_cols)

    part_x = down(hid_x, down_x, x)
    part_y = down(hid_y, down_y, y)
    sum_x = sum(
        (shift(part_x[d], "y", d) if d else part_x[0]).astype(F32) for d in range(4)
    ).astype(BF16)
    sum_y = sum(
        (shift(part_y[d], "x", d) if d else part_y[0]).astype(F32) for d in range(4)
    ).astype(BF16)
    expert_out = jnp.concatenate([sum_x, sum_y], axis=1)

    def refold(block):
        out = 0.0
        for i in range(QUARTERS):
            out = out + dot(unfold[i].T, block[:, i * QCOLS : (i + 1) * QCOLS])
        return out.astype(BF16).reshape(4, 48, QCOLS)

    back1, back2 = refold(expert_out[:48]), refold(expert_out[48:])
    returned = [None] * NZ
    for i, d in enumerate(NEAR):
        returned[d] = shift(back1[i], "z", -d) if d else back1[i]
    for i, d in enumerate(FAR):
        returned[d] = shift(back2[i], "z", -d)
    returned = jnp.stack(returned)
    kept = returned[:, :24].reshape(NZ * 24, QCOLS)
    given = shift(returned[:, 24:].reshape(NZ * 24, QCOLS), "c", 1)

    gates_rel = gates.reshape(TOK, NC, NZ).transpose(1, 2, 0)
    spread = jnp.broadcast_to(
        gates_rel[:, :, None, None, None, :], (NC, NZ, QUARTERS, CAP, QUARTERS, TOK)
    ).reshape(NC, NZ * QUARTERS * CAP, QUARTERS * TOK)
    weights = jnp.where(dispatch, spread, 0.0)
    combined = 0.0
    for rows, weight in ((kept, weights[0]), (given, weights[1])):
        for part in split_hi_lo(weight):
            combined = combined + lax.dot_general(
                part, rows, (((0,), (0,)), ((), ())), preferred_element_type=F32
            )
    combined = jnp.concatenate(
        [combined[i * TOK : (i + 1) * TOK] for i in range(QUARTERS)], axis=1
    )
    return (hidden + combined).astype(BF16)


def solution(mesh):
    grid = Mesh(mesh.devices.reshape(NX, NY, NZ, NC), ("x", "y", "z", "c"))
    seq, exp = ("x", "y"), ("z", "c")
    placed = (
        P(seq, exp),
        P(seq, exp),
        P(seq, exp),
        P(seq, exp),
        P(seq + exp, None),
        P(exp, None),
        P(),
        P(exp, None, seq),
        P(exp, None, seq),
        P(exp, seq, None),
        P(seq + exp, None),
    )
    return jax.shard_map(
        shards, mesh=grid, in_specs=placed, out_specs=P(seq + exp, None), check_vma=False
    )
```

```python
import jax
import jax.numpy as jnp
from jax import lax
from jax.experimental import pallas as pl
from jax.experimental.pallas import tpu as pltpu
from jax.sharding import Mesh, PartitionSpec as P

D = 3072
HEAD_DIM = 128
TOK = 32
CAP = 6
QUARTERS = 4
QCOLS = D // QUARTERS
NX, NY, NZ, NC = 4, 4, 8, 2
SIZES = {"x": NX, "y": NY, "z": NZ, "c": NC}
NEAR, FAR = (0, 1, 7, 2), (6, 3, 5, 4)
HIGHEST = lax.Precision.HIGHEST
F32, BF16 = jnp.float32, jnp.bfloat16


def shift(v, axis, by):
    n = SIZES[axis]
    return lax.ppermute(v, axis, [(i, (i + by) % n) for i in range(n)])


def swap(v, axis):
    return lax.ppermute(v, axis, [(i, i ^ 1) for i in range(SIZES[axis])])


def ahead(v, axis):
    return [v, shift(v, axis, -1), shift(v, axis, 2), shift(v, axis, 1)]


def ahead_split(v, axis):
    up, down = shift(v, axis, -1), shift(v, axis, 1)
    half = v.shape[0] // 2
    far = jnp.concatenate([shift(up[:half], axis, -1), shift(down[half:], axis, 1)], axis=0)
    return [v, up, far, down]


def dot(a, b):
    return jnp.dot(a, b, preferred_element_type=F32)


def split_hi_lo(v):
    hi = v.astype(BF16)
    return hi, (v - hi.astype(F32)).astype(BF16)


def pack(state, total):
    hi, lo = split_hi_lo(total)
    rows = jnp.stack([hi, lo], axis=1)[:, :, None]
    rows = jnp.broadcast_to(rows, (2, 2, HEAD_DIM))
    rows = jnp.concatenate([rows, jnp.zeros((2, 6, HEAD_DIM), BF16)], axis=1)
    return jnp.concatenate([state.astype(BF16), rows], axis=1)


def unpack(message):
    m = message.astype(F32)
    return m[:, :HEAD_DIM], m[:, HEAD_DIM, 0] + m[:, HEAD_DIM + 1, 0]


def fold(messages, own, place):
    states, totals = zip(own, *[unpack(m) for m in messages])
    where = [(place + SIZES["x"] - d) % 4 for d in range(4)]
    ordered = [sum(jnp.where(where[d] == j, totals[d], 0.0) for d in range(4)) for j in range(4)]
    before = jnp.zeros_like(states[0])
    everything = jnp.zeros_like(states[0])
    for d in range(4):
        till_here = sum(
            jnp.where((j > where[d]) & (j < place), ordered[j], 0.0) for j in range(4)
        )
        till_end = sum(jnp.where(j > where[d], ordered[j], 0.0) for j in range(4))
        weight = jnp.where(where[d] < place, jnp.exp(till_here), 0.0)
        before = before + weight[:, None, None] * states[d]
        everything = everything + jnp.exp(till_end)[:, None, None] * states[d]
    total_before = sum(jnp.where(j < place, ordered[j], 0.0) for j in range(4))
    return before, total_before, everything, sum(ordered)


def incoming(state, total):
    message = pack(state, total)
    row = [shift(message, "y", d) for d in (1, 2, 3)]
    before, total_before, everything, total_row = fold(
        row, (state, total), lax.axis_index("y")
    )
    message = pack(everything, total_row)
    rows = [shift(message, "x", d) for d in (1, 2, 3)]
    earlier, _, _, _ = fold(rows, (everything, total_row), lax.axis_index("x"))
    return before + jnp.exp(total_before)[:, None, None] * earlier


def attention(queries, keys, values, log_decay):
    rows = queries.shape[0]
    q = queries.reshape(rows, 2, HEAD_DIM)
    k = keys.reshape(rows, 2, HEAD_DIM)
    v = values.reshape(rows, 2, HEAD_DIM)
    cumulative = jnp.cumsum(log_decay, axis=0)
    tail = cumulative[-1]
    scaled_key = k.astype(F32) * jnp.exp(tail[None, :] - cumulative)[:, :, None]
    value_float = v.astype(F32)
    state = jnp.einsum("jhd,jhe->hde", scaled_key, value_float, precision=HIGHEST)
    state_in = incoming(state, tail)
    causal = jnp.arange(rows)[:, None] >= jnp.arange(rows)[None, :]
    differences = cumulative[:, None, :] - cumulative[None, :, :]
    damping = jnp.where(causal[:, :, None], jnp.exp(jnp.minimum(differences, 0.0)), 0.0)
    scores = jnp.einsum("ihd,jhd->ijh", q, k, preferred_element_type=F32)
    within = jnp.einsum("ijh,jhd->ihd", scores * damping, value_float, precision=HIGHEST)
    scaled_query = q.astype(F32) * jnp.exp(cumulative)[:, :, None]
    mixed = within + jnp.einsum("ihd,hde->ihe", scaled_query, state_in, precision=HIGHEST)
    scale = lax.rsqrt(jnp.mean(mixed * mixed, axis=-1, keepdims=True) + 1e-06)
    return (mixed * scale).astype(BF16).reshape(rows, 2 * HEAD_DIM)


def arrange_kernel(a_ref, b_ref, c_ref, *outs):
    first = [(a_ref, 0), (b_ref, 0), (c_ref, 0), (b_ref, 1)]
    second = [(a_ref, 1), (b_ref, 2), (c_ref, 1), (b_ref, 3)]
    for dx in range(4):
        for dy in range(4):
            ref, at = first[dy]
            one = ref[at * 192 + dx * 48 : at * 192 + dx * 48 + 48]
            ref, at = second[dx]
            two = ref[at * 192 + dy * 48 : at * 192 + dy * 48 + 48]
            outs[dx][dy * 96 : dy * 96 + 48] = one
            outs[dx][dy * 96 + 48 : dy * 96 + 96] = two
            outs[4 + dy][dx * 96 : dx * 96 + 48] = one
            outs[4 + dy][dx * 96 + 48 : dx * 96 + 96] = two


def arrange(a, b, c):
    units = a.shape[1]
    return pl.pallas_call(
        arrange_kernel,
        out_shape=[jax.ShapeDtypeStruct((384, units), BF16)] * 8,
        compiler_params=pltpu.CompilerParams(vmem_limit_bytes=32 << 20),
        cost_estimate=pl.CostEstimate(flops=0, bytes_accessed=4 << 20, transcendentals=0),
    )(a, b, c)


def down_kernel(place_ref, p0, p1, p2, p3, w_ref, out_ref):
    total = jnp.zeros(out_ref.shape, F32)
    for d, piece in enumerate((p0, p1, p2, p3)):
        total = total + dot(piece[...], w_ref[lax.rem(place_ref[0] + 4 - d, 4)])
    out_ref[...] = total.astype(BF16)


def down(pieces, weights, place):
    rows, units = pieces[0].shape
    cols, tile = weights.shape[2], 512
    whole = pl.BlockSpec((rows, units), lambda n, place: (0, 0))
    return pl.pallas_call(
        down_kernel,
        grid_spec=pltpu.PrefetchScalarGridSpec(
            num_scalar_prefetch=1,
            grid=(cols // tile,),
            in_specs=[whole] * 4
            + [pl.BlockSpec((4, units, tile), lambda n, place: (0, 0, n))],
            out_specs=pl.BlockSpec((rows, tile), lambda n, place: (0, n)),
        ),
        out_shape=jax.ShapeDtypeStruct((rows, cols), BF16),
        compiler_params=pltpu.CompilerParams(vmem_limit_bytes=32 << 20),
        cost_estimate=pl.CostEstimate(
            flops=8 * rows * units * cols, bytes_accessed=8 << 20, transcendentals=0
        ),
    )(place.astype(jnp.int32).reshape(1), *pieces, weights)


def unfold_matrix():
    row = jnp.arange(48)
    place, core, slot = row // 12, (row // 6) % 2, row % 6
    quarter = jnp.arange(QUARTERS)[:, None]
    source = place * 48 + core * 24 + quarter * 6 + slot
    return (source[:, :, None] == jnp.arange(192)[None, None, :]).astype(BF16)


def shards(
    queries, keys, values, log_decay, residual, out_weight, router, w_gate, w_up, w_down, routes
):
    z, c = lax.axis_index("z"), lax.axis_index("c")
    x, y = lax.axis_index("x"), lax.axis_index("y")
    half_cols = D // 2
    down_x = lax.all_gather(w_down[0][:, :half_cols], "x", axis=0)
    down_y = lax.all_gather(w_down[0][:, half_cols:], "y", axis=0)
    far_weight = swap(out_weight, "z")
    weight_near = jnp.concatenate([out_weight, swap(out_weight, "c")], axis=0)
    weight_far = jnp.concatenate([far_weight, swap(far_weight, "c")], axis=0)
    gate_up = jnp.concatenate([w_gate[0], w_up[0]], axis=1)

    ids = jnp.arange(16)
    relative = 2 * ((z + ids % NZ) % NZ) + (c ^ (ids // NZ))
    named = (routes[:, :, None] == relative[None, None, :]).any(axis=1)
    member = named.astype(F32)
    earlier = (jnp.arange(TOK)[:, None] > jnp.arange(TOK)[None, :]).astype(F32)
    slot = jnp.dot(earlier, member).astype(jnp.int32)
    router_rel = dot(
        router, (ids[:, None] == relative[None, :]).astype(BF16)
    ).astype(BF16)
    chosen = named[:, :, None] & (slot[:, :, None] == jnp.arange(CAP)[None, None, :])
    chosen = chosen.reshape(TOK, NC, NZ, CAP).transpose(1, 2, 3, 0)
    same = jnp.eye(QUARTERS, dtype=jnp.bool_)
    dispatch = chosen[:, :, None, :, None, :] & same[None, None, :, None, :, None]
    dispatch = dispatch.reshape(NC, NZ * QUARTERS * CAP, QUARTERS * TOK)
    dispatch_bf = dispatch.astype(BF16)

    heads = attention(queries, keys, values, log_decay).reshape(4, 2, NC, TOK, 2 * HEAD_DIM)
    pair, bit = z // 2, z % 2
    same_core = jnp.where(c == 0, heads[:, :, 0], heads[:, :, 1])
    other_core = jnp.where(c == 0, heads[:, :, 1], heads[:, :, 0])

    def by_bit(v):
        first, second = v[:, 0].reshape(128, -1), v[:, 1].reshape(128, -1)
        return jnp.where(bit == 0, first, second), jnp.where(bit == 0, second, first)

    own_here, own_there = by_bit(same_core)
    sib = swap(jnp.concatenate(by_bit(other_core), axis=0), "c")
    far_heads = swap(jnp.concatenate([own_there, sib[128:]], axis=1), "z")
    near_heads = jnp.concatenate([own_here, sib[:128]], axis=1)
    projected = dot(near_heads, weight_near) + dot(far_heads, weight_far)
    projected = projected.astype(BF16).reshape(4, TOK, D)
    attn = lax.dynamic_index_in_dim(projected, pair, 0, keepdims=False).astype(F32)
    parts = [
        shift(lax.dynamic_index_in_dim(projected, (pair + d) % 4, 0, keepdims=False), "z", 2 * d)
        for d in (2, 1, 3)
    ]
    for part in parts:
        attn = attn + part.astype(F32)
    hidden = residual.astype(F32) + attn
    normed = (hidden * lax.rsqrt(jnp.mean(hidden * hidden, axis=-1, keepdims=True) + 1e-06)).astype(
        BF16
    )
    logits = dot(normed, router_rel)
    picked = jax.nn.sigmoid(logits) * member
    gates = picked / jnp.sum(picked, axis=1, keepdims=True)

    folded = jnp.concatenate(
        [normed[:, i * QCOLS : (i + 1) * QCOLS] for i in range(QUARTERS)], axis=0
    )
    keep = dot(dispatch_bf[0], folded).astype(BF16).reshape(NZ, 24, QCOLS)
    give = shift(dot(dispatch_bf[1], folded).astype(BF16), "c", 1).reshape(NZ, 24, QCOLS)
    leaving = jnp.concatenate([keep, give], axis=1)
    arrived = {d: (shift(leaving[d], "z", d) if d else leaving[0]) for d in NEAR + FAR}
    unfold = unfold_matrix()

    def unfolded(places):
        block = jnp.concatenate([arrived[d] for d in places], axis=0)
        return jnp.concatenate(
            [dot(unfold[i], block).astype(BF16) for i in range(QUARTERS)], axis=1
        )

    first, second = unfolded(NEAR), unfolded(FAR)
    rows_x, rows_y = lax.optimization_barrier(
        (jnp.concatenate(ahead(first, "x"), axis=0), jnp.concatenate(ahead(second, "y"), axis=0))
    )
    by_y, by_x = ahead_split(rows_x, "y"), ahead_split(rows_y, "x")

    def expert_hidden(blocks):
        product = dot(jnp.concatenate(blocks, axis=0), gate_up)
        gate_part, up_part = jnp.split(product, 2, axis=1)
        return (jax.nn.silu(gate_part) * up_part).astype(BF16)

    hidden_a = expert_hidden([by_y[0], by_x[0]])
    hidden_b = expert_hidden([by_y[1], by_y[3], by_x[1], by_x[3]])
    hidden_c = expert_hidden([by_y[2], by_x[2]])
    sends = arrange(hidden_a, hidden_b, hidden_c)
    hid_x = [sends[0]] + [shift(sends[d], "x", d) for d in (1, 2, 3)]
    hid_y = [sends[4]] + [shift(sends[4 + d], "y", d) for d in (1, 2, 3)]
    part_x = down(hid_x, down_x, x).reshape(4, 96, half_cols)
    part_y = down(hid_y, down_y, y).reshape(4, 96, half_cols)
    sum_x = sum(
        (shift(part_x[d], "y", d) if d else part_x[0]).astype(F32) for d in range(4)
    ).astype(BF16)
    sum_y = sum(
        (shift(part_y[d], "x", d) if d else part_y[0]).astype(F32) for d in range(4)
    ).astype(BF16)
    expert_out = jnp.concatenate([sum_x, sum_y], axis=1)

    def refold(block):
        out = 0.0
        for i in range(QUARTERS):
            out = out + dot(unfold[i].T, block[:, i * QCOLS : (i + 1) * QCOLS])
        return out.astype(BF16).reshape(4, 48, QCOLS)

    back1, back2 = refold(expert_out[:48]), refold(expert_out[48:])
    returned = [None] * NZ
    for i, d in enumerate(NEAR):
        returned[d] = shift(back1[i], "z", -d) if d else back1[i]
    for i, d in enumerate(FAR):
        returned[d] = shift(back2[i], "z", -d)
    returned = jnp.stack(returned)
    kept = returned[:, :24].reshape(NZ * 24, QCOLS)
    given = shift(returned[:, 24:].reshape(NZ * 24, QCOLS), "c", 1)

    gates_rel = gates.reshape(TOK, NC, NZ).transpose(1, 2, 0)
    spread = jnp.broadcast_to(
        gates_rel[:, :, None, None, None, :], (NC, NZ, QUARTERS, CAP, QUARTERS, TOK)
    ).reshape(NC, NZ * QUARTERS * CAP, QUARTERS * TOK)
    weights = jnp.where(dispatch, spread, 0.0)
    combined = 0.0
    for rows, weight in ((kept, weights[0]), (given, weights[1])):
        for part in split_hi_lo(weight):
            combined = combined + lax.dot_general(
                part, rows, (((0,), (0,)), ((), ())), preferred_element_type=F32
            )
    combined = jnp.concatenate(
        [combined[i * TOK : (i + 1) * TOK] for i in range(QUARTERS)], axis=1
    )
    return (hidden + combined).astype(BF16)


def solution(mesh):
    grid = Mesh(mesh.devices.reshape(NX, NY, NZ, NC), ("x", "y", "z", "c"))
    seq, exp = ("x", "y"), ("z", "c")
    placed = (
        P(seq, exp),
        P(seq, exp),
        P(seq, exp),
        P(seq, exp),
        P(seq + exp, None),
        P(exp, None),
        P(),
        P(exp, None, seq),
        P(exp, None, seq),
        P(exp, seq, None),
        P(seq + exp, None),
    )
    return jax.shard_map(
        shards, mesh=grid, in_specs=placed, out_specs=P(seq + exp, None), check_vma=False
    )
```

```python
import jax
import jax.numpy as jnp
from jax import lax
from jax.experimental import pallas as pl
from jax.experimental.pallas import tpu as pltpu
from jax.sharding import Mesh, PartitionSpec as P

D = 3072
HEAD_DIM = 128
TOK = 32
CAP = 6
QUARTERS = 4
QCOLS = D // QUARTERS
NX, NY, NZ, NC = 4, 4, 8, 2
SIZES = {"x": NX, "y": NY, "z": NZ, "c": NC}
NEAR, FAR = (0, 1, 7, 2), (6, 3, 5, 4)
HIGHEST = lax.Precision.HIGHEST
F32, BF16 = jnp.float32, jnp.bfloat16


def shift(v, axis, by):
    n = SIZES[axis]
    return lax.ppermute(v, axis, [(i, (i + by) % n) for i in range(n)])


def swap(v, axis):
    return lax.ppermute(v, axis, [(i, i ^ 1) for i in range(SIZES[axis])])


def ahead(v, axis):
    return [v, shift(v, axis, -1), shift(v, axis, 2), shift(v, axis, 1)]


def ahead_split(v, axis):
    up, down = shift(v, axis, -1), shift(v, axis, 1)
    half = v.shape[0] // 2
    far = jnp.concatenate([shift(up[:half], axis, -1), shift(down[half:], axis, 1)], axis=0)
    return [v, up, far, down]


def dot(a, b):
    return jnp.dot(a, b, preferred_element_type=F32)


def split_hi_lo(v):
    hi = v.astype(BF16)
    return hi, (v - hi.astype(F32)).astype(BF16)


def pack(state, total):
    hi, lo = split_hi_lo(total)
    rows = jnp.stack([hi, lo], axis=1)[:, :, None]
    rows = jnp.broadcast_to(rows, (2, 2, HEAD_DIM))
    rows = jnp.concatenate([rows, jnp.zeros((2, 6, HEAD_DIM), BF16)], axis=1)
    return jnp.concatenate([state.astype(BF16), rows], axis=1)


def unpack(message):
    m = message.astype(F32)
    return m[:, :HEAD_DIM], m[:, HEAD_DIM, 0] + m[:, HEAD_DIM + 1, 0]


def fold(messages, own, place):
    states, totals = zip(own, *[unpack(m) for m in messages])
    where = [(place + SIZES["x"] - d) % 4 for d in range(4)]
    ordered = [sum(jnp.where(where[d] == j, totals[d], 0.0) for d in range(4)) for j in range(4)]
    before = jnp.zeros_like(states[0])
    everything = jnp.zeros_like(states[0])
    for d in range(4):
        till_here = sum(
            jnp.where((j > where[d]) & (j < place), ordered[j], 0.0) for j in range(4)
        )
        till_end = sum(jnp.where(j > where[d], ordered[j], 0.0) for j in range(4))
        weight = jnp.where(where[d] < place, jnp.exp(till_here), 0.0)
        before = before + weight[:, None, None] * states[d]
        everything = everything + jnp.exp(till_end)[:, None, None] * states[d]
    total_before = sum(jnp.where(j < place, ordered[j], 0.0) for j in range(4))
    return before, total_before, everything, sum(ordered)


def incoming(state, total):
    message = pack(state, total)
    row = [shift(message, "y", d) for d in (1, 2, 3)]
    before, total_before, everything, total_row = fold(
        row, (state, total), lax.axis_index("y")
    )
    message = pack(everything, total_row)
    rows = [shift(message, "x", d) for d in (1, 2, 3)]
    earlier, _, _, _ = fold(rows, (everything, total_row), lax.axis_index("x"))
    return before + jnp.exp(total_before)[:, None, None] * earlier


def attention(queries, keys, values, log_decay):
    rows = queries.shape[0]
    q = queries.reshape(rows, 2, HEAD_DIM)
    k = keys.reshape(rows, 2, HEAD_DIM)
    v = values.reshape(rows, 2, HEAD_DIM)
    cumulative = jnp.cumsum(log_decay, axis=0)
    tail = cumulative[-1]
    scaled_key = k.astype(F32) * jnp.exp(tail[None, :] - cumulative)[:, :, None]
    value_float = v.astype(F32)
    state = jnp.einsum("jhd,jhe->hde", scaled_key, value_float, precision=HIGHEST)
    state_in = incoming(state, tail)
    causal = jnp.arange(rows)[:, None] >= jnp.arange(rows)[None, :]
    differences = cumulative[:, None, :] - cumulative[None, :, :]
    damping = jnp.where(causal[:, :, None], jnp.exp(jnp.minimum(differences, 0.0)), 0.0)
    scores = jnp.einsum("ihd,jhd->ijh", q, k, preferred_element_type=F32)
    within = jnp.einsum("ijh,jhd->ihd", scores * damping, value_float, precision=HIGHEST)
    scaled_query = q.astype(F32) * jnp.exp(cumulative)[:, :, None]
    mixed = within + jnp.einsum("ihd,hde->ihe", scaled_query, state_in, precision=HIGHEST)
    scale = lax.rsqrt(jnp.mean(mixed * mixed, axis=-1, keepdims=True) + 1e-06)
    return (mixed * scale).astype(BF16).reshape(rows, 2 * HEAD_DIM)


def arrange_kernel(a_ref, b_ref, c_ref, *outs):
    first = [(a_ref, 0), (b_ref, 0), (c_ref, 0), (b_ref, 1)]
    second = [(a_ref, 1), (b_ref, 2), (c_ref, 1), (b_ref, 3)]
    for dx in range(4):
        for dy in range(4):
            ref, at = first[dy]
            outs[dx][dy * 96 : dy * 96 + 48] = ref[at * 192 + dx * 48 : at * 192 + dx * 48 + 48]
            ref, at = second[dx]
            outs[dx][dy * 96 + 48 : dy * 96 + 96] = ref[
                at * 192 + dy * 48 : at * 192 + dy * 48 + 48
            ]


def arrange(a, b, c):
    units = a.shape[1]
    return pl.pallas_call(
        arrange_kernel,
        out_shape=[jax.ShapeDtypeStruct((384, units), BF16)] * 4,
        compiler_params=pltpu.CompilerParams(vmem_limit_bytes=6 << 20),
        cost_estimate=pl.CostEstimate(flops=0, bytes_accessed=2 << 20, transcendentals=0),
    )(a, b, c)


def down_kernel(place_ref, p0, p1, p2, p3, w_ref, o0, o1, o2, o3, held):
    units = p0.shape[1]

    @pl.when(pl.program_id(0) == 0)
    def _():
        for d, piece in enumerate((p0, p1, p2, p3)):
            at = lax.rem(place_ref[0] + 4 - d, 4)
            held[:, pl.ds(pl.multiple_of(at * units, 128), units)] = piece[...]

    for i, out in enumerate((o0, o1, o2, o3)):
        if i % 2 == 0:
            total = dot(held[i * 96 : i * 96 + 192], w_ref[...]).astype(BF16)
        out[...] = total[i % 2 * 96 : i % 2 * 96 + 96]


def down(pieces, weights, place):
    rows, units = pieces[0].shape
    deep, cols = weights.shape
    tile = 512
    whole = pl.BlockSpec((rows, units), lambda n, place: (0, 0))
    return pl.pallas_call(
        down_kernel,
        grid_spec=pltpu.PrefetchScalarGridSpec(
            num_scalar_prefetch=1,
            grid=(cols // tile,),
            in_specs=[whole] * 4 + [pl.BlockSpec((deep, tile), lambda n, place: (0, n))],
            out_specs=[pl.BlockSpec((96, tile), lambda n, place: (0, n))] * 4,
            scratch_shapes=[pltpu.VMEM((rows, deep), BF16)],
        ),
        out_shape=[jax.ShapeDtypeStruct((96, cols), BF16)] * 4,
        compiler_params=pltpu.CompilerParams(vmem_limit_bytes=12 << 20),
        cost_estimate=pl.CostEstimate(
            flops=2 * rows * deep * cols, bytes_accessed=13 << 20, transcendentals=0
        ),
    )(place.astype(jnp.int32).reshape(1), *pieces, weights)


def refold_kernel(p0, p1, p2, p3, fold_ref, *outs):
    for half in range(2):
        at = slice(half * 48, half * 48 + 48)
        total = sum(p[at].astype(F32) for p in (p0, p1, p2, p3)).astype(BF16)
        rows = 0.0
        for i in range(QUARTERS):
            rows = rows + dot(fold_ref[i], total[:, i * QCOLS : (i + 1) * QCOLS])
        rows = rows.astype(BF16)
        for i in range(4):
            outs[half * 4 + i][...] = rows[i * 48 : i * 48 + 48]


def refold(parts, fold):
    return pl.pallas_call(
        refold_kernel,
        out_shape=[jax.ShapeDtypeStruct((48, QCOLS), BF16)] * NZ,
        compiler_params=pltpu.CompilerParams(vmem_limit_bytes=12 << 20),
        cost_estimate=pl.CostEstimate(flops=2 << 27, bytes_accessed=3 << 20, transcendentals=0),
    )(*parts, fold)


def unfold_matrix():
    row = jnp.arange(48)
    place, core, slot = row // 12, (row // 6) % 2, row % 6
    quarter = jnp.arange(QUARTERS)[:, None]
    source = place * 48 + core * 24 + quarter * 6 + slot
    return (source[:, :, None] == jnp.arange(192)[None, None, :]).astype(BF16)


def shards(
    queries, keys, values, log_decay, residual, out_weight, router, w_gate, w_up, w_down, routes
):
    z, c = lax.axis_index("z"), lax.axis_index("c")
    x = lax.axis_index("x")
    down_all = lax.all_gather(w_down[0], "x", axis=0, tiled=True)
    weight_pair = jnp.concatenate([out_weight, swap(out_weight, "c")], axis=0)
    gate_up = jnp.concatenate([w_gate[0], w_up[0]], axis=1)

    ids = jnp.arange(16)
    relative = 2 * ((z + ids % NZ) % NZ) + (c ^ (ids // NZ))
    named = (routes[:, :, None] == relative[None, None, :]).any(axis=1)
    member = named.astype(F32)
    earlier = (jnp.arange(TOK)[:, None] > jnp.arange(TOK)[None, :]).astype(F32)
    slot = jnp.dot(earlier, member).astype(jnp.int32)
    router_rel = dot(
        router, (ids[:, None] == relative[None, :]).astype(BF16)
    ).astype(BF16)
    chosen = named[:, :, None] & (slot[:, :, None] == jnp.arange(CAP)[None, None, :])
    chosen = chosen.reshape(TOK, NC, NZ, CAP).transpose(1, 2, 3, 0)
    same = jnp.eye(QUARTERS, dtype=jnp.bool_)
    dispatch = chosen[:, :, None, :, None, :] & same[None, None, :, None, :, None]
    dispatch = dispatch.reshape(NC, NZ * QUARTERS * CAP, QUARTERS * TOK)
    dispatch_bf = dispatch.astype(BF16)

    heads_out = attention(queries, keys, values, log_decay).reshape(NZ, NC, TOK, 2 * HEAD_DIM)
    mine = jnp.where(c == 0, heads_out[:, 0], heads_out[:, 1]).reshape(NZ * TOK, 2 * HEAD_DIM)
    theirs = jnp.where(c == 0, heads_out[:, 1], heads_out[:, 0]).reshape(NZ * TOK, 2 * HEAD_DIM)
    both = jnp.concatenate([mine, swap(theirs, "c")], axis=1)
    projected = dot(both, weight_pair).astype(BF16).reshape(NZ, TOK, D)
    attn = lax.dynamic_index_in_dim(projected, z, 0, keepdims=False).astype(F32)
    parts = [
        shift(lax.dynamic_index_in_dim(projected, (z + d) % NZ, 0, keepdims=False), "z", d)
        for d in (1, 7, 2, 6, 3, 5, 4)
    ]
    for part in parts:
        attn = attn + part.astype(F32)
    hidden = residual.astype(F32) + attn
    normed = (hidden * lax.rsqrt(jnp.mean(hidden * hidden, axis=-1, keepdims=True) + 1e-06)).astype(
        BF16
    )
    logits = dot(normed, router_rel)
    picked = jax.nn.sigmoid(logits) * member
    gates = picked / jnp.sum(picked, axis=1, keepdims=True)

    folded = jnp.concatenate(
        [normed[:, i * QCOLS : (i + 1) * QCOLS] for i in range(QUARTERS)], axis=0
    )
    keep = dot(dispatch_bf[0], folded).astype(BF16).reshape(NZ, 24, QCOLS)
    give = shift(dot(dispatch_bf[1], folded).astype(BF16), "c", 1).reshape(NZ, 24, QCOLS)
    leaving = jnp.concatenate([keep, give], axis=1)
    arrived = {d: (shift(leaving[d], "z", d) if d else leaving[0]) for d in NEAR + FAR}
    unfold = unfold_matrix()

    def unfolded(places):
        block = jnp.concatenate([arrived[d] for d in places], axis=0)
        return jnp.concatenate(
            [dot(unfold[i], block).astype(BF16) for i in range(QUARTERS)], axis=1
        )

    first, second = unfolded(NEAR), unfolded(FAR)
    rows_x, rows_y = lax.optimization_barrier(
        (jnp.concatenate(ahead(first, "x"), axis=0), jnp.concatenate(ahead(second, "y"), axis=0))
    )
    by_y, by_x = ahead_split(rows_x, "y"), ahead_split(rows_y, "x")

    def expert_hidden(blocks):
        product = dot(jnp.concatenate(blocks, axis=0), gate_up)
        gate_part, up_part = jnp.split(product, 2, axis=1)
        return (jax.nn.silu(gate_part) * up_part).astype(BF16)

    hidden_a = expert_hidden([by_y[0], by_x[0]])
    hidden_b = expert_hidden([by_y[1], by_y[3], by_x[1], by_x[3]])
    hidden_c = expert_hidden([by_y[2], by_x[2]])
    sends = arrange(hidden_a, hidden_b, hidden_c)
    pieces = [sends[0]] + [shift(sends[d], "x", d) for d in (1, 2, 3)]
    partial = down(pieces, down_all, x)
    parts = [partial[0]] + [shift(partial[d], "y", d) for d in (1, 2, 3)]
    back = refold(parts, unfold.transpose(0, 2, 1))
    returned = [None] * NZ
    for d in (1, 7, 2, 6, 3, 5, 4):
        returned[d] = shift(back[(NEAR + FAR).index(d)], "z", -d)
    returned[0] = back[0]
    returned = jnp.stack(returned)
    kept = returned[:, :24].reshape(NZ * 24, QCOLS)
    given = shift(returned[:, 24:].reshape(NZ * 24, QCOLS), "c", 1)

    gates_rel = gates.reshape(TOK, NC, NZ).transpose(1, 2, 0)
    spread = jnp.broadcast_to(
        gates_rel[:, :, None, None, None, :], (NC, NZ, QUARTERS, CAP, QUARTERS, TOK)
    ).reshape(NC, NZ * QUARTERS * CAP, QUARTERS * TOK)
    weights = jnp.where(dispatch, spread, 0.0)
    combined = 0.0
    for rows, weight in ((kept, weights[0]), (given, weights[1])):
        for part in split_hi_lo(weight):
            combined = combined + lax.dot_general(
                part, rows, (((0,), (0,)), ((), ())), preferred_element_type=F32
            )
    combined = jnp.concatenate(
        [combined[i * TOK : (i + 1) * TOK] for i in range(QUARTERS)], axis=1
    )
    return (hidden + combined).astype(BF16)


def solution(mesh):
    grid = Mesh(mesh.devices.reshape(NX, NY, NZ, NC), ("x", "y", "z", "c"))
    seq, exp = ("x", "y"), ("z", "c")
    placed = (
        P(seq, exp),
        P(seq, exp),
        P(seq, exp),
        P(seq, exp),
        P(seq + exp, None),
        P(exp, None),
        P(),
        P(exp, None, seq),
        P(exp, None, seq),
        P(exp, seq, None),
        P(seq + exp, None),
    )
    return jax.shard_map(
        shards, mesh=grid, in_specs=placed, out_specs=P(seq + exp, None), check_vma=False
    )
```

```python
import jax
import jax.numpy as jnp
from jax import lax
from jax.experimental import pallas as pl
from jax.experimental.pallas import tpu as pltpu
from jax.sharding import Mesh, PartitionSpec as P

D = 3072
HEAD_DIM = 128
TOK = 32
CAP = 6
QUARTERS = 4
QCOLS = D // QUARTERS
NX, NY, NZ, NC = 4, 4, 8, 2
SIZES = {"x": NX, "y": NY, "z": NZ, "c": NC}
NEAR, FAR = (0, 1, 7, 2), (6, 3, 5, 4)
F32, BF16 = jnp.float32, jnp.bfloat16


def shift(v, axis, by):
    n = SIZES[axis]
    return lax.ppermute(v, axis, [(i, (i + by) % n) for i in range(n)])


def swap(v, axis):
    return lax.ppermute(v, axis, [(i, i ^ 1) for i in range(SIZES[axis])])


def ahead(v, axis):
    return [v, shift(v, axis, -1), shift(v, axis, 2), shift(v, axis, 1)]


def ahead_split(v, axis):
    up, down = shift(v, axis, -1), shift(v, axis, 1)
    half = v.shape[0] // 2
    far = jnp.concatenate([shift(up[:half], axis, -1), shift(down[half:], axis, 1)], axis=0)
    return [v, up, far, down]


def dot(a, b):
    return jnp.dot(a, b, preferred_element_type=F32)


def split_hi_lo(v):
    hi = v.astype(BF16)
    return hi, (v - hi.astype(F32)).astype(BF16)


MSG = HEAD_DIM + 16


def parts_of(v):
    hi, rest = split_hi_lo(v)
    mid = (v - hi.astype(F32)).astype(BF16)
    return hi, mid, (v - hi.astype(F32) - mid.astype(F32)).astype(BF16)


def message_rows(total):
    hi, lo = split_hi_lo(total)
    row = lax.broadcasted_iota(jnp.int32, (16, HEAD_DIM), 0)
    rows = jnp.where(row == 0, hi.astype(F32), jnp.where(row == 1, lo.astype(F32), 0.0))
    return rows.astype(BF16)


def state_kernel(k_ref, v_ref, decay_ref, message_ref, col_ref, row_ref):
    rows = k_ref.shape[0]
    lane = lax.broadcasted_iota(jnp.int32, (rows, HEAD_DIM), 1)
    decay = jnp.where(lane < 64, decay_ref[:, 0:1], decay_ref[:, 1:2])
    tri = (
        lax.broadcasted_iota(jnp.int32, (rows, rows), 0)
        >= lax.broadcasted_iota(jnp.int32, (rows, rows), 1)
    ).astype(F32).astype(BF16)
    col, row = 0.0, 0.0
    for part in parts_of(decay):
        col = col + dot(tri, part)
        row = row + lax.dot_general(
            part, tri, (((0,), (1,)), ((), ())), preferred_element_type=F32
        )
    col_ref[...] = col
    for h in range(2):
        row_ref[h * 8 : h * 8 + 8] = row[h * 64 : h * 64 + 8]
        cols = slice(h * HEAD_DIM, (h + 1) * HEAD_DIM)
        here = jnp.broadcast_to(col[:, h * 64 : h * 64 + 1], (rows, HEAD_DIM))
        tail = here[rows - 1 : rows]
        scaled = k_ref[:, cols].astype(F32) * jnp.exp(tail - here)
        state = 0.0
        for part in split_hi_lo(scaled):
            state = state + lax.dot_general(
                part, v_ref[:, cols], (((0,), (0,)), ((), ())), preferred_element_type=F32
            )
        message_ref[h, :HEAD_DIM] = state.astype(BF16)
        message_ref[h, HEAD_DIM:] = message_rows(tail)


def within_kernel(q_ref, k_ref, v_ref, col_ref, row_ref, out_ref):
    rows = q_ref.shape[0]
    step = 256
    for h in range(2):
        cols = slice(h * HEAD_DIM, (h + 1) * HEAD_DIM)
        for start in range(0, rows, step):
            stop = start + step
            scores = lax.dot_general(
                q_ref[start:stop, cols],
                k_ref[:stop, cols],
                (((1,), (1,)), ((), ())),
                preferred_element_type=F32,
            )
            apart = col_ref[start:stop, h * 64 : h * 64 + 1] - row_ref[h * 8 : h * 8 + 1, :stop]
            causal = start + lax.broadcasted_iota(
                jnp.int32, (step, stop), 0
            ) >= lax.broadcasted_iota(jnp.int32, (step, stop), 1)
            damped = scores * jnp.where(causal, jnp.exp(jnp.minimum(apart, 0.0)), 0.0)
            total = 0.0
            for part in split_hi_lo(damped):
                total = total + dot(part, v_ref[:stop, cols])
            out_ref[start:stop, cols] = total


def fold(messages, h, place):
    totals = [m[h, HEAD_DIM:].astype(F32) for m in messages]
    totals = [t[0:1] + t[1:2] for t in totals]
    states = [m[h, :HEAD_DIM].astype(F32) for m in messages]
    where = [lax.rem(place + 4 - d, 4) for d in range(4)]
    ordered = [sum(jnp.where(where[d] == j, totals[d], 0.0) for d in range(4)) for j in range(4)]
    before, everything = 0.0, 0.0
    for d in range(4):
        till_here = sum(
            jnp.where((j > where[d]) & (j < place), ordered[j], 0.0) for j in range(4)
        )
        till_end = sum(jnp.where(j > where[d], ordered[j], 0.0) for j in range(4))
        before = before + jnp.where(where[d] < place, jnp.exp(till_here), 0.0) * states[d]
        everything = everything + jnp.exp(till_end) * states[d]
    total_before = sum(jnp.where(j < place, ordered[j], 0.0) for j in range(4))
    return before, total_before, everything, sum(ordered)


def fold_kernel(place_ref, m0, m1, m2, m3, message_ref, before_ref):
    for h in range(2):
        before, total_before, everything, total = fold((m0, m1, m2, m3), h, place_ref[0])
        before_ref[h, :HEAD_DIM] = before
        before_ref[h, HEAD_DIM:] = jnp.broadcast_to(jnp.exp(total_before), (8, HEAD_DIM))
        message_ref[h, :HEAD_DIM] = everything.astype(BF16)
        message_ref[h, HEAD_DIM:] = message_rows(total)


def mix_kernel(
    place_ref, m0, m1, m2, m3, before_ref, q_ref, col_ref, within_ref, mine_ref, other_ref, held
):
    for h in range(2):
        cols = slice(h * HEAD_DIM, (h + 1) * HEAD_DIM)
        earlier, _, _, _ = fold((m0, m1, m2, m3), h, place_ref[0])
        state = before_ref[h, :HEAD_DIM] + before_ref[h, HEAD_DIM : HEAD_DIM + 1] * earlier
        carried = 0.0
        for part in split_hi_lo(state):
            carried = carried + dot(q_ref[:, cols], part)
        mixed = within_ref[:, cols] + jnp.exp(col_ref[:, h * 64 : h * 64 + 1]) * carried
        scale = lax.rsqrt(jnp.mean(mixed * mixed, axis=-1, keepdims=True) + 1e-06)
        held[:, cols] = (mixed * scale).astype(BF16)
    core = place_ref[1]
    for i in range(NZ):
        at = pl.multiple_of(i * 2 * TOK + core * TOK, TOK)
        mine_ref[i * TOK : (i + 1) * TOK] = held[pl.ds(at, TOK)]
        at = pl.multiple_of(i * 2 * TOK + (1 - core) * TOK, TOK)
        other_ref[i * TOK : (i + 1) * TOK] = held[pl.ds(at, TOK)]


def local_kernel(body, outs, scalars=(), scratch=(), flops=1 << 27, grant=16):
    vmem = pl.BlockSpec(memory_space=pltpu.VMEM)
    smem = pl.BlockSpec(memory_space=pltpu.SMEM)

    def call(*operands):
        given = (jnp.stack([s.astype(jnp.int32) for s in scalars]),) if scalars else ()
        return pl.pallas_call(
            body,
            out_shape=[jax.ShapeDtypeStruct(*o) for o in outs],
            in_specs=[smem] * len(given) + [vmem] * len(operands),
            out_specs=[vmem] * len(outs),
            scratch_shapes=list(scratch),
            compiler_params=pltpu.CompilerParams(vmem_limit_bytes=grant << 20),
            cost_estimate=pl.CostEstimate(
                flops=flops, bytes_accessed=2 << 20, transcendentals=1 << 18
            ),
        )(*given, *operands)

    return call


def state_call(keys, values, log_decay):
    rows = keys.shape[0]
    return local_kernel(
        state_kernel,
        [((2, MSG, HEAD_DIM), BF16), ((rows, HEAD_DIM), F32), ((16, rows), F32)],
        flops=1 << 28,
    )(keys, values, log_decay)


def within_call(queries, keys, values, col, row):
    return local_kernel(within_kernel, [(queries.shape, F32)], flops=1 << 29)(
        queries, keys, values, col, row
    )[0]


def fold_call(messages, place):
    return local_kernel(
        fold_kernel,
        [((2, MSG, HEAD_DIM), BF16), ((2, HEAD_DIM + 8, HEAD_DIM), F32)],
        scalars=(place,),
    )(*messages)


def mix_call(messages, before, queries, col, within, place, core):
    rows, cols = queries.shape
    return local_kernel(
        mix_kernel,
        [((rows // 2, cols), BF16)] * 2,
        scalars=(place, core),
        scratch=[pltpu.VMEM((rows, cols), BF16)],
    )(*messages, before, queries, col, within)


def attention(queries, keys, values, log_decay):
    message, col, row = state_call(keys, values, log_decay)
    messages = [message] + [shift(message, "y", d) for d in (1, 2, 3)]
    within = within_call(queries, keys, values, col, row)
    message, before = fold_call(messages, lax.axis_index("y"))
    messages = [message] + [shift(message, "x", d) for d in (1, 2, 3)]
    return mix_call(
        messages, before, queries, col, within, lax.axis_index("x"), lax.axis_index("c")
    )


def arrange_kernel(a_ref, b_ref, c_ref, *outs):
    first = [(a_ref, 0), (b_ref, 0), (c_ref, 0), (b_ref, 1)]
    second = [(a_ref, 1), (b_ref, 2), (c_ref, 1), (b_ref, 3)]
    for dx in range(4):
        for dy in range(4):
            ref, at = first[dy]
            outs[dx][dy * 96 : dy * 96 + 48] = ref[at * 192 + dx * 48 : at * 192 + dx * 48 + 48]
            ref, at = second[dx]
            outs[dx][dy * 96 + 48 : dy * 96 + 96] = ref[
                at * 192 + dy * 48 : at * 192 + dy * 48 + 48
            ]


def arrange(a, b, c):
    units = a.shape[1]
    return pl.pallas_call(
        arrange_kernel,
        out_shape=[jax.ShapeDtypeStruct((384, units), BF16)] * 4,
        compiler_params=pltpu.CompilerParams(vmem_limit_bytes=6 << 20),
        cost_estimate=pl.CostEstimate(flops=0, bytes_accessed=2 << 20, transcendentals=0),
    )(a, b, c)


def down_kernel(place_ref, p0, p1, p2, p3, w_ref, o0, o1, o2, o3, held, tiles, sems):
    units = p0.shape[1]
    width = tiles.shape[2]
    count = w_ref.shape[1] // width

    def fetch(n):
        return pltpu.make_async_copy(
            w_ref.at[:, n * width : (n + 1) * width], tiles.at[n % 2], sems.at[n % 2]
        )

    fetch(0).start()
    for d, piece in enumerate((p0, p1, p2, p3)):
        at = lax.rem(place_ref[0] + 4 - d, 4)
        held[:, pl.ds(pl.multiple_of(at * units, 128), units)] = piece[...]
    for n in range(count):
        if n + 1 < count:
            fetch(n + 1).start()
        fetch(n).wait()
        total = dot(held[...], tiles[n % 2]).astype(BF16)
        for i, out in enumerate((o0, o1, o2, o3)):
            out[:, n * width : (n + 1) * width] = total[i * 96 : i * 96 + 96]


def down(pieces, weights, place):
    rows, units = pieces[0].shape
    deep, cols = weights.shape
    vmem = pl.BlockSpec(memory_space=pltpu.VMEM)
    return pl.pallas_call(
        down_kernel,
        in_specs=[pl.BlockSpec(memory_space=pltpu.SMEM)]
        + [vmem] * 4
        + [pl.BlockSpec(memory_space=pltpu.HBM)],
        out_specs=[vmem] * 4,
        scratch_shapes=[
            pltpu.VMEM((rows, deep), BF16),
            pltpu.VMEM((2, deep, 512), BF16),
            pltpu.SemaphoreType.DMA((2,)),
        ],
        out_shape=[jax.ShapeDtypeStruct((96, cols), BF16)] * 4,
        compiler_params=pltpu.CompilerParams(vmem_limit_bytes=16 << 20),
        cost_estimate=pl.CostEstimate(
            flops=2 * rows * deep * cols, bytes_accessed=13 << 20, transcendentals=0
        ),
    )(place.astype(jnp.int32).reshape(1), *pieces, weights)


def refold_kernel(p0, p1, p2, p3, fold_ref, *outs):
    for half in range(2):
        at = slice(half * 48, half * 48 + 48)
        total = sum(p[at].astype(F32) for p in (p0, p1, p2, p3)).astype(BF16)
        rows = 0.0
        for i in range(QUARTERS):
            rows = rows + dot(fold_ref[i], total[:, i * QCOLS : (i + 1) * QCOLS])
        rows = rows.astype(BF16)
        for i in range(4):
            outs[half * 4 + i][...] = rows[i * 48 : i * 48 + 48]


def refold(parts, fold):
    return pl.pallas_call(
        refold_kernel,
        out_shape=[jax.ShapeDtypeStruct((48, QCOLS), BF16)] * NZ,
        compiler_params=pltpu.CompilerParams(vmem_limit_bytes=12 << 20),
        cost_estimate=pl.CostEstimate(flops=2 << 27, bytes_accessed=3 << 20, transcendentals=0),
    )(*parts, fold)


def unfold_matrix():
    row = jnp.arange(48)
    place, core, slot = row // 12, (row // 6) % 2, row % 6
    quarter = jnp.arange(QUARTERS)[:, None]
    source = place * 48 + core * 24 + quarter * 6 + slot
    return (source[:, :, None] == jnp.arange(192)[None, None, :]).astype(BF16)


def shards(
    queries, keys, values, log_decay, residual, out_weight, router, w_gate, w_up, w_down, routes
):
    z, c = lax.axis_index("z"), lax.axis_index("c")
    x = lax.axis_index("x")
    down_all = lax.all_gather(w_down[0], "x", axis=0, tiled=True)
    weight_pair = jnp.concatenate([out_weight, swap(out_weight, "c")], axis=0)
    gate_up = jnp.concatenate([w_gate[0], w_up[0]], axis=1)

    ids = jnp.arange(16)
    relative = 2 * ((z + ids % NZ) % NZ) + (c ^ (ids // NZ))
    named = (routes[:, :, None] == relative[None, None, :]).any(axis=1)
    member = named.astype(F32)
    earlier = (jnp.arange(TOK)[:, None] > jnp.arange(TOK)[None, :]).astype(F32)
    slot = jnp.dot(earlier, member).astype(jnp.int32)
    router_rel = dot(
        router, (ids[:, None] == relative[None, :]).astype(BF16)
    ).astype(BF16)
    chosen = named[:, :, None] & (slot[:, :, None] == jnp.arange(CAP)[None, None, :])
    chosen = chosen.reshape(TOK, NC, NZ, CAP).transpose(1, 2, 3, 0)
    same = jnp.eye(QUARTERS, dtype=jnp.bool_)
    dispatch = chosen[:, :, None, :, None, :] & same[None, None, :, None, :, None]
    dispatch = dispatch.reshape(NC, NZ * QUARTERS * CAP, QUARTERS * TOK)
    dispatch_bf = dispatch.astype(BF16)

    mine, theirs = attention(queries, keys, values, log_decay)
    both = jnp.concatenate([mine, swap(theirs, "c")], axis=1)
    projected = dot(both, weight_pair).astype(BF16).reshape(NZ, TOK, D)
    attn = lax.dynamic_index_in_dim(projected, z, 0, keepdims=False).astype(F32)
    parts = [
        shift(lax.dynamic_index_in_dim(projected, (z + d) % NZ, 0, keepdims=False), "z", d)
        for d in (1, 7, 2, 6, 3, 5, 4)
    ]
    for part in parts:
        attn = attn + part.astype(F32)
    hidden = residual.astype(F32) + attn
    normed = (hidden * lax.rsqrt(jnp.mean(hidden * hidden, axis=-1, keepdims=True) + 1e-06)).astype(
        BF16
    )
    logits = dot(normed, router_rel)
    picked = jax.nn.sigmoid(logits) * member
    gates = picked / jnp.sum(picked, axis=1, keepdims=True)

    folded = jnp.concatenate(
        [normed[:, i * QCOLS : (i + 1) * QCOLS] for i in range(QUARTERS)], axis=0
    )
    keep = dot(dispatch_bf[0], folded).astype(BF16).reshape(NZ, 24, QCOLS)
    give = shift(dot(dispatch_bf[1], folded).astype(BF16), "c", 1).reshape(NZ, 24, QCOLS)
    leaving = jnp.concatenate([keep, give], axis=1)
    arrived = {d: (shift(leaving[d], "z", d) if d else leaving[0]) for d in NEAR + FAR}
    unfold = unfold_matrix()

    def unfolded(places):
        block = jnp.concatenate([arrived[d] for d in places], axis=0)
        return jnp.concatenate(
            [dot(unfold[i], block).astype(BF16) for i in range(QUARTERS)], axis=1
        )

    first, second = unfolded(NEAR), unfolded(FAR)
    rows_x, rows_y = lax.optimization_barrier(
        (jnp.concatenate(ahead(first, "x"), axis=0), jnp.concatenate(ahead(second, "y"), axis=0))
    )
    by_y, by_x = ahead_split(rows_x, "y"), ahead_split(rows_y, "x")

    def expert_hidden(blocks):
        product = dot(jnp.concatenate(blocks, axis=0), gate_up)
        gate_part, up_part = jnp.split(product, 2, axis=1)
        return (jax.nn.silu(gate_part) * up_part).astype(BF16)

    hidden_a = expert_hidden([by_y[0], by_x[0]])
    hidden_b = expert_hidden([by_y[1], by_y[3], by_x[1], by_x[3]])
    hidden_c = expert_hidden([by_y[2], by_x[2]])
    sends = arrange(hidden_a, hidden_b, hidden_c)
    pieces = [sends[0]] + [shift(sends[d], "x", d) for d in (1, 2, 3)]
    partial = down(pieces, down_all, x)
    parts = [partial[0]] + [shift(partial[d], "y", d) for d in (1, 2, 3)]
    back = refold(parts, unfold.transpose(0, 2, 1))
    returned = [None] * NZ
    for d in (1, 7, 2, 6, 3, 5, 4):
        returned[d] = shift(back[(NEAR + FAR).index(d)], "z", -d)
    returned[0] = back[0]
    returned = jnp.stack(returned)
    kept = returned[:, :24].reshape(NZ * 24, QCOLS)
    given = shift(returned[:, 24:].reshape(NZ * 24, QCOLS), "c", 1)

    gates_rel = gates.reshape(TOK, NC, NZ).transpose(1, 2, 0)
    spread = jnp.broadcast_to(
        gates_rel[:, :, None, None, None, :], (NC, NZ, QUARTERS, CAP, QUARTERS, TOK)
    ).reshape(NC, NZ * QUARTERS * CAP, QUARTERS * TOK)
    weights = jnp.where(dispatch, spread, 0.0)
    combined = 0.0
    for rows, weight in ((kept, weights[0]), (given, weights[1])):
        for part in split_hi_lo(weight):
            combined = combined + lax.dot_general(
                part, rows, (((0,), (0,)), ((), ())), preferred_element_type=F32
            )
    combined = jnp.concatenate(
        [combined[i * TOK : (i + 1) * TOK] for i in range(QUARTERS)], axis=1
    )
    return (hidden + combined).astype(BF16)


def solution(mesh):
    grid = Mesh(mesh.devices.reshape(NX, NY, NZ, NC), ("x", "y", "z", "c"))
    seq, exp = ("x", "y"), ("z", "c")
    placed = (
        P(seq, exp),
        P(seq, exp),
        P(seq, exp),
        P(seq, exp),
        P(seq + exp, None),
        P(exp, None),
        P(),
        P(exp, None, seq),
        P(exp, None, seq),
        P(exp, seq, None),
        P(seq + exp, None),
    )
    return jax.shard_map(
        shards, mesh=grid, in_specs=placed, out_specs=P(seq + exp, None), check_vma=False
    )
```

```python
import jax
import jax.numpy as jnp
from jax import lax
from jax.experimental import pallas as pl
from jax.experimental.pallas import tpu as pltpu
from jax.sharding import Mesh, PartitionSpec as P

D = 3072
HEAD_DIM = 128
TOK = 32
CAP = 6
QUARTERS = 4
QCOLS = D // QUARTERS
NX, NY, NZ, NC = 4, 4, 8, 2
SIZES = {"x": NX, "y": NY, "z": NZ, "c": NC}
F32, BF16 = jnp.float32, jnp.bfloat16


def shift(v, axis, by):
    n = SIZES[axis]
    return lax.ppermute(v, axis, [(i, (i + by) % n) for i in range(n)])


def part_ways(v, by, back=False):
    pairs = []
    for z in range(NZ):
        for c in range(NC):
            there = (z + (1 - 2 * c) * by) % NZ
            pairs.append((z * NC + c, there * NC + c))
    if back:
        pairs = [(there, here) for here, there in pairs]
    return lax.ppermute(v, ("z", "c"), pairs)


def swap(v, axis):
    return lax.ppermute(v, axis, [(i, i ^ 1) for i in range(SIZES[axis])])


def ahead(v, axis):
    return [v, shift(v, axis, -1), shift(v, axis, 2), shift(v, axis, 1)]


def ahead_split(v, axis):
    up, down = shift(v, axis, -1), shift(v, axis, 1)
    half = v.shape[0] // 2
    far = jnp.concatenate([shift(up[:half], axis, -1), shift(down[half:], axis, 1)], axis=0)
    return [v, up, far, down]


def dot(a, b):
    return jnp.dot(a, b, preferred_element_type=F32)


def split_hi_lo(v):
    hi = v.astype(BF16)
    return hi, (v - hi.astype(F32)).astype(BF16)


MSG = HEAD_DIM + 16


def parts_of(v):
    hi, rest = split_hi_lo(v)
    mid = (v - hi.astype(F32)).astype(BF16)
    return hi, mid, (v - hi.astype(F32) - mid.astype(F32)).astype(BF16)


def message_rows(total):
    hi, lo = split_hi_lo(total)
    row = lax.broadcasted_iota(jnp.int32, (16, HEAD_DIM), 0)
    rows = jnp.where(row == 0, hi.astype(F32), jnp.where(row == 1, lo.astype(F32), 0.0))
    return rows.astype(BF16)


def state_kernel(k_ref, v_ref, decay_ref, message_ref, col_ref, row_ref):
    rows = k_ref.shape[0]
    lane = lax.broadcasted_iota(jnp.int32, (rows, HEAD_DIM), 1)
    decay = jnp.where(lane < 64, decay_ref[:, 0:1], decay_ref[:, 1:2])
    tri = (
        lax.broadcasted_iota(jnp.int32, (rows, rows), 0)
        >= lax.broadcasted_iota(jnp.int32, (rows, rows), 1)
    ).astype(F32).astype(BF16)
    col, row = 0.0, 0.0
    for part in parts_of(decay):
        col = col + dot(tri, part)
        row = row + lax.dot_general(
            part, tri, (((0,), (1,)), ((), ())), preferred_element_type=F32
        )
    col_ref[...] = col
    for h in range(2):
        row_ref[h * 8 : h * 8 + 8] = row[h * 64 : h * 64 + 8]
        cols = slice(h * HEAD_DIM, (h + 1) * HEAD_DIM)
        here = jnp.broadcast_to(col[:, h * 64 : h * 64 + 1], (rows, HEAD_DIM))
        tail = here[rows - 1 : rows]
        scaled = k_ref[:, cols].astype(F32) * jnp.exp(tail - here)
        state = 0.0
        for part in split_hi_lo(scaled):
            state = state + lax.dot_general(
                part, v_ref[:, cols], (((0,), (0,)), ((), ())), preferred_element_type=F32
            )
        message_ref[h, :HEAD_DIM] = state.astype(BF16)
        message_ref[h, HEAD_DIM:] = message_rows(tail)


def within_kernel(q_ref, k_ref, v_ref, col_ref, row_ref, out_ref):
    rows = q_ref.shape[0]
    step = 256
    for h in range(2):
        cols = slice(h * HEAD_DIM, (h + 1) * HEAD_DIM)
        for start in range(0, rows, step):
            stop = start + step
            scores = lax.dot_general(
                q_ref[start:stop, cols],
                k_ref[:stop, cols],
                (((1,), (1,)), ((), ())),
                preferred_element_type=F32,
            )
            apart = col_ref[start:stop, h * 64 : h * 64 + 1] - row_ref[h * 8 : h * 8 + 1, :stop]
            causal = start + lax.broadcasted_iota(
                jnp.int32, (step, stop), 0
            ) >= lax.broadcasted_iota(jnp.int32, (step, stop), 1)
            damped = scores * jnp.where(causal, jnp.exp(jnp.minimum(apart, 0.0)), 0.0)
            total = 0.0
            for part in split_hi_lo(damped):
                total = total + dot(part, v_ref[:stop, cols])
            out_ref[start:stop, cols] = total


def fold(messages, h, place):
    totals = [m[h, HEAD_DIM:].astype(F32) for m in messages]
    totals = [t[0:1] + t[1:2] for t in totals]
    states = [m[h, :HEAD_DIM].astype(F32) for m in messages]
    where = [lax.rem(place + 4 - d, 4) for d in range(4)]
    ordered = [sum(jnp.where(where[d] == j, totals[d], 0.0) for d in range(4)) for j in range(4)]
    before, everything = 0.0, 0.0
    for d in range(4):
        till_here = sum(
            jnp.where((j > where[d]) & (j < place), ordered[j], 0.0) for j in range(4)
        )
        till_end = sum(jnp.where(j > where[d], ordered[j], 0.0) for j in range(4))
        before = before + jnp.where(where[d] < place, jnp.exp(till_here), 0.0) * states[d]
        everything = everything + jnp.exp(till_end) * states[d]
    total_before = sum(jnp.where(j < place, ordered[j], 0.0) for j in range(4))
    return before, total_before, everything, sum(ordered)


def fold_kernel(place_ref, m0, m1, m2, m3, message_ref, before_ref):
    for h in range(2):
        before, total_before, everything, total = fold((m0, m1, m2, m3), h, place_ref[0])
        before_ref[h, :HEAD_DIM] = before
        before_ref[h, HEAD_DIM:] = jnp.broadcast_to(jnp.exp(total_before), (8, HEAD_DIM))
        message_ref[h, :HEAD_DIM] = everything.astype(BF16)
        message_ref[h, HEAD_DIM:] = message_rows(total)


def mix_kernel(
    place_ref, m0, m1, m2, m3, before_ref, q_ref, col_ref, within_ref, mine_ref, other_ref, held
):
    for h in range(2):
        cols = slice(h * HEAD_DIM, (h + 1) * HEAD_DIM)
        earlier, _, _, _ = fold((m0, m1, m2, m3), h, place_ref[0])
        state = before_ref[h, :HEAD_DIM] + before_ref[h, HEAD_DIM : HEAD_DIM + 1] * earlier
        carried = 0.0
        for part in split_hi_lo(state):
            carried = carried + dot(q_ref[:, cols], part)
        mixed = within_ref[:, cols] + jnp.exp(col_ref[:, h * 64 : h * 64 + 1]) * carried
        scale = lax.rsqrt(jnp.mean(mixed * mixed, axis=-1, keepdims=True) + 1e-06)
        held[:, cols] = (mixed * scale).astype(BF16)
    core, z = place_ref[1], place_ref[2]
    for out, carrier in ((mine_ref, core), (other_ref, 1 - core)):
        sign = 1 - 2 * carrier
        for j in (1, 2, 3):
            at = pl.multiple_of(lax.rem(z + NZ + sign * j, NZ) * 2 * TOK, TOK)
            out[(j - 1) * 2 * TOK : j * 2 * TOK] = held[pl.ds(at, 2 * TOK)]
        for row, chip in ((6 * TOK, lax.rem(z + 4, NZ)), (7 * TOK, z)):
            at = pl.multiple_of(chip * 2 * TOK + carrier * TOK, TOK)
            out[row : row + TOK] = held[pl.ds(at, TOK)]


def project_kernel(mine_ref, got_ref, own_ref, sib_ref, *outs):
    tile = 512

    def step(n, carry):
        cols = pl.ds(pl.multiple_of(n * tile, tile), tile)
        total = dot(mine_ref[...], own_ref[:, cols]) + dot(got_ref[...], sib_ref[:, cols])
        total = total.astype(BF16)
        row = 0
        for out in outs:
            out[:, cols] = total[row : row + out.shape[0]]
            row += out.shape[0]
        return carry

    lax.fori_loop(0, D // tile, step, 0)


def local_kernel(body, outs, scalars=(), scratch=(), flops=1 << 27, grant=16):
    vmem = pl.BlockSpec(memory_space=pltpu.VMEM)
    smem = pl.BlockSpec(memory_space=pltpu.SMEM)

    def call(*operands):
        given = (jnp.stack([s.astype(jnp.int32) for s in scalars]),) if scalars else ()
        return pl.pallas_call(
            body,
            out_shape=[jax.ShapeDtypeStruct(*o) for o in outs],
            in_specs=[smem] * len(given) + [vmem] * len(operands),
            out_specs=[vmem] * len(outs),
            scratch_shapes=list(scratch),
            compiler_params=pltpu.CompilerParams(vmem_limit_bytes=grant << 20),
            cost_estimate=pl.CostEstimate(
                flops=flops, bytes_accessed=2 << 20, transcendentals=1 << 18
            ),
        )(*given, *operands)

    return call


def state_call(keys, values, log_decay):
    rows = keys.shape[0]
    return local_kernel(
        state_kernel,
        [((2, MSG, HEAD_DIM), BF16), ((rows, HEAD_DIM), F32), ((16, rows), F32)],
        flops=1 << 28,
    )(keys, values, log_decay)


def within_call(queries, keys, values, col, row):
    return local_kernel(within_kernel, [(queries.shape, F32)], flops=1 << 29)(
        queries, keys, values, col, row
    )[0]


def fold_call(messages, place):
    return local_kernel(
        fold_kernel,
        [((2, MSG, HEAD_DIM), BF16), ((2, HEAD_DIM + 8, HEAD_DIM), F32)],
        scalars=(place,),
    )(*messages)


def mix_call(messages, before, queries, col, within, place, core, z):
    rows, cols = queries.shape
    return local_kernel(
        mix_kernel,
        [((rows // 2, cols), BF16)] * 2,
        scalars=(place, core, z),
        scratch=[pltpu.VMEM((rows, cols), BF16)],
    )(*messages, before, queries, col, within)


def attention(queries, keys, values, log_decay):
    message, col, row = state_call(keys, values, log_decay)
    messages = [message] + [shift(message, "y", d) for d in (1, 2, 3)]
    within = within_call(queries, keys, values, col, row)
    message, before = fold_call(messages, lax.axis_index("y"))
    messages = [message] + [shift(message, "x", d) for d in (1, 2, 3)]
    places = [lax.axis_index(a) for a in ("x", "c", "z")]
    return mix_call(messages, before, queries, col, within, *places)


def arrange_kernel(a_ref, b_ref, c_ref, *outs):
    first = [(a_ref, 0), (b_ref, 0), (c_ref, 0), (b_ref, 1)]
    second = [(a_ref, 1), (b_ref, 2), (c_ref, 1), (b_ref, 3)]
    for dx in range(4):
        for dy in range(4):
            ref, at = first[dy]
            outs[dx][dy * 96 : dy * 96 + 48] = ref[at * 192 + dx * 48 : at * 192 + dx * 48 + 48]
            ref, at = second[dx]
            outs[dx][dy * 96 + 48 : dy * 96 + 96] = ref[
                at * 192 + dy * 48 : at * 192 + dy * 48 + 48
            ]


def arrange(a, b, c):
    units = a.shape[1]
    return pl.pallas_call(
        arrange_kernel,
        out_shape=[jax.ShapeDtypeStruct((384, units), BF16)] * 4,
        compiler_params=pltpu.CompilerParams(vmem_limit_bytes=6 << 20),
        cost_estimate=pl.CostEstimate(flops=0, bytes_accessed=2 << 20, transcendentals=0),
    )(a, b, c)


def down_kernel(place_ref, p0, p1, p2, p3, w_ref, o0, o1, o2, o3, held, tiles, sems):
    units = p0.shape[1]
    width = tiles.shape[2]
    count = w_ref.shape[1] // width

    def fetch(n):
        return pltpu.make_async_copy(
            w_ref.at[:, n * width : (n + 1) * width], tiles.at[n % 2], sems.at[n % 2]
        )

    fetch(0).start()
    for d, piece in enumerate((p0, p1, p2, p3)):
        at = lax.rem(place_ref[0] + 4 - d, 4)
        held[:, pl.ds(pl.multiple_of(at * units, 128), units)] = piece[...]
    for n in range(count):
        if n + 1 < count:
            fetch(n + 1).start()
        fetch(n).wait()
        total = dot(held[...], tiles[n % 2]).astype(BF16)
        for i, out in enumerate((o0, o1, o2, o3)):
            out[:, n * width : (n + 1) * width] = total[i * 96 : i * 96 + 96]


def down(pieces, weights, place):
    rows, units = pieces[0].shape
    deep, cols = weights.shape
    vmem = pl.BlockSpec(memory_space=pltpu.VMEM)
    return pl.pallas_call(
        down_kernel,
        in_specs=[pl.BlockSpec(memory_space=pltpu.SMEM)]
        + [vmem] * 4
        + [pl.BlockSpec(memory_space=pltpu.HBM)],
        out_specs=[vmem] * 4,
        scratch_shapes=[
            pltpu.VMEM((rows, deep), BF16),
            pltpu.VMEM((2, deep, 512), BF16),
            pltpu.SemaphoreType.DMA((2,)),
        ],
        out_shape=[jax.ShapeDtypeStruct((96, cols), BF16)] * 4,
        compiler_params=pltpu.CompilerParams(vmem_limit_bytes=56 << 20),
        cost_estimate=pl.CostEstimate(
            flops=2 * rows * deep * cols, bytes_accessed=13 << 20, transcendentals=0
        ),
    )(place.astype(jnp.int32).reshape(1), *pieces, weights)


def refold_kernel(p0, p1, p2, p3, fold_ref, *outs):
    for half in range(2):
        at = slice(half * 48, half * 48 + 48)
        total = sum(p[at].astype(F32) for p in (p0, p1, p2, p3)).astype(BF16)
        rows = 0.0
        for i in range(QUARTERS):
            rows = rows + dot(fold_ref[i], total[:, i * QCOLS : (i + 1) * QCOLS])
        rows = rows.astype(BF16)
        row = 0
        for out in outs[:4] if half == 0 else outs[4:]:
            out[...] = rows[row : row + out.shape[0]]
            row += out.shape[0]


def refold(parts, fold):
    return pl.pallas_call(
        refold_kernel,
        out_shape=[jax.ShapeDtypeStruct((n, QCOLS), BF16) for n in (48, 48, 48, 48, 144, 48)],
        compiler_params=pltpu.CompilerParams(vmem_limit_bytes=12 << 20),
        cost_estimate=pl.CostEstimate(flops=2 << 27, bytes_accessed=3 << 20, transcendentals=0),
    )(*parts, fold)


def unfold_matrix():
    row = jnp.arange(48)
    place, core, slot = row // 12, (row // 6) % 2, row % 6
    quarter = jnp.arange(QUARTERS)[:, None]
    source = place * 48 + core * 24 + quarter * 6 + slot
    return (source[:, :, None] == jnp.arange(192)[None, None, :]).astype(BF16)


def shards(
    queries, keys, values, log_decay, residual, out_weight, router, w_gate, w_up, w_down, routes
):
    z, c = lax.axis_index("z"), lax.axis_index("c")
    x = lax.axis_index("x")
    down_all = lax.all_gather(w_down[0], "x", axis=0, tiled=True)
    weight_sib = swap(out_weight, "c")
    gate_up = jnp.concatenate([w_gate[0], w_up[0]], axis=1)

    ids = jnp.arange(16)
    carrier = c ^ (ids // 8)
    kind = ids % 8
    away = jnp.where(kind < 6, (1 - 2 * carrier) * (kind // 2 + 1), jnp.where(kind == 6, 4, 0))
    crossed = jnp.where(kind < 6, kind % 2, 0)
    relative = 2 * ((z + away + NZ) % NZ) + (carrier ^ crossed)
    named = (routes[:, :, None] == relative[None, None, :]).any(axis=1)
    member = named.astype(F32)
    earlier = (jnp.arange(TOK)[:, None] > jnp.arange(TOK)[None, :]).astype(F32)
    slot = jnp.dot(earlier, member).astype(jnp.int32)
    router_rel = dot(
        router, (ids[:, None] == relative[None, :]).astype(BF16)
    ).astype(BF16)
    chosen = named[:, :, None] & (slot[:, :, None] == jnp.arange(CAP)[None, None, :])
    chosen = chosen.reshape(TOK, NC, NZ, CAP).transpose(1, 2, 3, 0)
    same = jnp.eye(QUARTERS, dtype=jnp.bool_)
    dispatch = chosen[:, :, None, :, None, :] & same[None, None, :, None, :, None]
    dispatch = dispatch.reshape(NC, NZ * QUARTERS * CAP, QUARTERS * TOK)
    dispatch_bf = dispatch.astype(BF16)

    mine, theirs = attention(queries, keys, values, log_decay)
    *leave, local = local_kernel(
        project_kernel,
        [((2 * TOK, D), BF16)] * 3 + [((TOK, D), BF16)] * 2,
        flops=1 << 30,
    )(mine, swap(theirs, "c"), out_weight, weight_sib)
    came = [part_ways(leave[j], j + 1) for j in range(4)]
    chip_sum = came[0].astype(F32) + came[1].astype(F32) + came[2].astype(F32)
    low, high = chip_sum[:TOK], chip_sum[TOK:]
    sibling_sum = swap(jnp.where(c == 0, high, low).astype(BF16), "c")
    attn = jnp.where(c == 0, low, high) + came[3].astype(F32) + local.astype(F32)
    attn = attn + sibling_sum.astype(F32)
    hidden = residual.astype(F32) + attn
    normed = (hidden * lax.rsqrt(jnp.mean(hidden * hidden, axis=-1, keepdims=True) + 1e-06)).astype(
        BF16
    )
    logits = dot(normed, router_rel)
    picked = jax.nn.sigmoid(logits) * member
    gates = picked / jnp.sum(picked, axis=1, keepdims=True)

    folded = jnp.concatenate(
        [normed[:, i * QCOLS : (i + 1) * QCOLS] for i in range(QUARTERS)], axis=0
    )
    keep = dot(dispatch_bf[0], folded).astype(BF16).reshape(8, 24, QCOLS)
    got = swap(dot(dispatch_bf[1], folded).astype(BF16), "c").reshape(8, 24, QCOLS)
    out_rows = [
        jnp.concatenate([keep[2 * j], got[2 * j], keep[2 * j + 1], got[2 * j + 1]], axis=0)
        for j in range(3)
    ]
    opposite = jnp.concatenate([keep[6], got[6]], axis=0)
    stayed = jnp.concatenate([keep[7], got[7]], axis=0)
    arrived = [part_ways(out_rows[j], j + 1) for j in range(3)]
    opposite = part_ways(opposite, 4)
    crossing = swap(jnp.concatenate([v[48:] for v in arrived], axis=0), "c")
    unfold = unfold_matrix()

    def unfolded(blocks):
        block = jnp.concatenate(blocks, axis=0)
        return jnp.concatenate(
            [dot(unfold[i], block).astype(BF16) for i in range(QUARTERS)], axis=1
        )

    first = unfolded([v[:48] for v in arrived] + [stayed])
    second = unfolded([crossing, opposite])
    rows_x, rows_y = lax.optimization_barrier(
        (jnp.concatenate(ahead(first, "x"), axis=0), jnp.concatenate(ahead(second, "y"), axis=0))
    )
    by_y, by_x = ahead_split(rows_x, "y"), ahead_split(rows_y, "x")

    def expert_hidden(blocks):
        product = dot(jnp.concatenate(blocks, axis=0), gate_up)
        gate_part, up_part = jnp.split(product, 2, axis=1)
        return (jax.nn.silu(gate_part) * up_part).astype(BF16)

    hidden_a = expert_hidden([by_y[0], by_x[0]])
    hidden_b = expert_hidden([by_y[1], by_y[3], by_x[1], by_x[3]])
    hidden_c = expert_hidden([by_y[2], by_x[2]])
    sends = arrange(hidden_a, hidden_b, hidden_c)
    pieces = [sends[0]] + [shift(sends[d], "x", d) for d in (1, 2, 3)]
    partial = down(pieces, down_all, x)
    parts = [partial[0]] + [shift(partial[d], "y", d) for d in (1, 2, 3)]
    own1, own2, own3, stayed, crossing, opposite = refold(parts, unfold.transpose(0, 2, 1))
    crossing = swap(crossing, "c")
    home = [
        part_ways(jnp.concatenate([own, crossing[48 * j : 48 * j + 48]], axis=0), j + 1, True)
        for j, own in enumerate((own1, own2, own3))
    ]
    opposite = part_ways(opposite, 4, True)
    kept = [v[at : at + 24] for v in home for at in (0, 48)] + [opposite[:24], stayed[:24]]
    given = [v[at : at + 24] for v in home for at in (24, 72)] + [opposite[24:], stayed[24:]]
    kept = jnp.concatenate(kept, axis=0)
    given = swap(jnp.concatenate(given, axis=0), "c")

    gates_rel = gates.reshape(TOK, NC, NZ).transpose(1, 2, 0)
    spread = jnp.broadcast_to(
        gates_rel[:, :, None, None, None, :], (NC, NZ, QUARTERS, CAP, QUARTERS, TOK)
    ).reshape(NC, NZ * QUARTERS * CAP, QUARTERS * TOK)
    weights = jnp.where(dispatch, spread, 0.0)
    combined = 0.0
    for rows, weight in ((kept, weights[0]), (given, weights[1])):
        for part in split_hi_lo(weight):
            combined = combined + lax.dot_general(
                part, rows, (((0,), (0,)), ((), ())), preferred_element_type=F32
            )
    combined = jnp.concatenate(
        [combined[i * TOK : (i + 1) * TOK] for i in range(QUARTERS)], axis=1
    )
    return (hidden + combined).astype(BF16)


def solution(mesh):
    grid = Mesh(mesh.devices.reshape(NX, NY, NZ, NC), ("x", "y", "z", "c"))
    seq, exp = ("x", "y"), ("z", "c")
    placed = (
        P(seq, exp),
        P(seq, exp),
        P(seq, exp),
        P(seq, exp),
        P(seq + exp, None),
        P(exp, None),
        P(),
        P(exp, None, seq),
        P(exp, None, seq),
        P(exp, seq, None),
        P(seq + exp, None),
    )
    return jax.shard_map(
        shards, mesh=grid, in_specs=placed, out_specs=P(seq + exp, None), check_vma=False
    )
```

```python
import jax
import jax.numpy as jnp
from jax import lax
from jax.experimental import pallas as pl
from jax.experimental.pallas import tpu as pltpu
from jax.sharding import Mesh, PartitionSpec as P

D = 3072
HEAD_DIM = 128
TOK = 32
CAP = 6
QUARTERS = 4
QCOLS = D // QUARTERS
NX, NY, NZ, NC = 4, 4, 8, 2
SIZES = {"x": NX, "y": NY, "z": NZ, "c": NC}
F32, BF16 = jnp.float32, jnp.bfloat16


def shift(v, axis, by):
    n = SIZES[axis]
    return lax.ppermute(v, axis, [(i, (i + by) % n) for i in range(n)])


def part_ways(v, by, back=False):
    pairs = []
    for z in range(NZ):
        for c in range(NC):
            there = (z + (1 - 2 * c) * by) % NZ
            pairs.append((z * NC + c, there * NC + c))
    if back:
        pairs = [(there, here) for here, there in pairs]
    return lax.ppermute(v, ("z", "c"), pairs)


def swap(v, axis):
    return lax.ppermute(v, axis, [(i, i ^ 1) for i in range(SIZES[axis])])


def ahead(v, axis):
    return [v, shift(v, axis, -1), shift(v, axis, 2), shift(v, axis, 1)]


def ahead_split(v, axis):
    up, down = shift(v, axis, -1), shift(v, axis, 1)
    half = v.shape[0] // 2
    far = jnp.concatenate([shift(up[:half], axis, -1), shift(down[half:], axis, 1)], axis=0)
    return [v, up, far, down]


def dot(a, b):
    return jnp.dot(a, b, preferred_element_type=F32)


def split_hi_lo(v):
    hi = v.astype(BF16)
    return hi, (v - hi.astype(F32)).astype(BF16)


MSG = HEAD_DIM + 16


def parts_of(v):
    hi, rest = split_hi_lo(v)
    mid = (v - hi.astype(F32)).astype(BF16)
    return hi, mid, (v - hi.astype(F32) - mid.astype(F32)).astype(BF16)


def message_rows(total):
    hi, lo = split_hi_lo(total)
    row = lax.broadcasted_iota(jnp.int32, (16, HEAD_DIM), 0)
    rows = jnp.where(row == 0, hi.astype(F32), jnp.where(row == 1, lo.astype(F32), 0.0))
    return rows.astype(BF16)


def state_kernel(k_ref, v_ref, decay_ref, message_ref, col_ref, row_ref):
    rows = k_ref.shape[0]
    lane = lax.broadcasted_iota(jnp.int32, (rows, HEAD_DIM), 1)
    decay = jnp.where(lane < 64, decay_ref[:, 0:1], decay_ref[:, 1:2])
    tri = (
        lax.broadcasted_iota(jnp.int32, (rows, rows), 0)
        >= lax.broadcasted_iota(jnp.int32, (rows, rows), 1)
    ).astype(F32).astype(BF16)
    col, row = 0.0, 0.0
    for part in parts_of(decay):
        col = col + dot(tri, part)
        row = row + lax.dot_general(
            part, tri, (((0,), (1,)), ((), ())), preferred_element_type=F32
        )
    col_ref[...] = col
    for h in range(2):
        row_ref[h * 8 : h * 8 + 8] = row[h * 64 : h * 64 + 8]
        cols = slice(h * HEAD_DIM, (h + 1) * HEAD_DIM)
        here = jnp.broadcast_to(col[:, h * 64 : h * 64 + 1], (rows, HEAD_DIM))
        tail = here[rows - 1 : rows]
        scaled = k_ref[:, cols].astype(F32) * jnp.exp(tail - here)
        state = 0.0
        for part in split_hi_lo(scaled):
            state = state + lax.dot_general(
                part, v_ref[:, cols], (((0,), (0,)), ((), ())), preferred_element_type=F32
            )
        message_ref[h, :HEAD_DIM] = state.astype(BF16)
        message_ref[h, HEAD_DIM:] = message_rows(tail)


def within_kernel(q_ref, k_ref, v_ref, col_ref, row_ref, out_ref):
    rows = q_ref.shape[0]
    step = 256
    for h in range(2):
        cols = slice(h * HEAD_DIM, (h + 1) * HEAD_DIM)
        for start in range(0, rows, step):
            stop = start + step
            scores = lax.dot_general(
                q_ref[start:stop, cols],
                k_ref[:stop, cols],
                (((1,), (1,)), ((), ())),
                preferred_element_type=F32,
            )
            apart = col_ref[start:stop, h * 64 : h * 64 + 1] - row_ref[h * 8 : h * 8 + 1, :stop]
            causal = start + lax.broadcasted_iota(
                jnp.int32, (step, stop), 0
            ) >= lax.broadcasted_iota(jnp.int32, (step, stop), 1)
            damped = scores * jnp.where(causal, jnp.exp(jnp.minimum(apart, 0.0)), 0.0)
            total = 0.0
            for part in split_hi_lo(damped):
                total = total + dot(part, v_ref[:stop, cols])
            out_ref[start:stop, cols] = total


def fold(messages, h, place):
    totals = [m[h, HEAD_DIM:].astype(F32) for m in messages]
    totals = [t[0:1] + t[1:2] for t in totals]
    states = [m[h, :HEAD_DIM].astype(F32) for m in messages]
    where = [lax.rem(place + 4 - d, 4) for d in range(4)]
    ordered = [sum(jnp.where(where[d] == j, totals[d], 0.0) for d in range(4)) for j in range(4)]
    before, everything = 0.0, 0.0
    for d in range(4):
        till_here = sum(
            jnp.where((j > where[d]) & (j < place), ordered[j], 0.0) for j in range(4)
        )
        till_end = sum(jnp.where(j > where[d], ordered[j], 0.0) for j in range(4))
        before = before + jnp.where(where[d] < place, jnp.exp(till_here), 0.0) * states[d]
        everything = everything + jnp.exp(till_end) * states[d]
    total_before = sum(jnp.where(j < place, ordered[j], 0.0) for j in range(4))
    return before, total_before, everything, sum(ordered)


def fold_kernel(place_ref, m0, m1, m2, m3, message_ref, before_ref):
    for h in range(2):
        before, total_before, everything, total = fold((m0, m1, m2, m3), h, place_ref[0])
        before_ref[h, :HEAD_DIM] = before
        before_ref[h, HEAD_DIM:] = jnp.broadcast_to(jnp.exp(total_before), (8, HEAD_DIM))
        message_ref[h, :HEAD_DIM] = everything.astype(BF16)
        message_ref[h, HEAD_DIM:] = message_rows(total)


def mix_kernel(
    place_ref, m0, m1, m2, m3, before_ref, q_ref, col_ref, within_ref, mine_ref, other_ref, held
):
    for h in range(2):
        cols = slice(h * HEAD_DIM, (h + 1) * HEAD_DIM)
        earlier, _, _, _ = fold((m0, m1, m2, m3), h, place_ref[0])
        state = before_ref[h, :HEAD_DIM] + before_ref[h, HEAD_DIM : HEAD_DIM + 1] * earlier
        carried = 0.0
        for part in split_hi_lo(state):
            carried = carried + dot(q_ref[:, cols], part)
        mixed = within_ref[:, cols] + jnp.exp(col_ref[:, h * 64 : h * 64 + 1]) * carried
        scale = lax.rsqrt(jnp.mean(mixed * mixed, axis=-1, keepdims=True) + 1e-06)
        held[:, cols] = (mixed * scale).astype(BF16)
    core = place_ref[1]
    for i in range(NZ):
        at = pl.multiple_of(i * 2 * TOK + core * TOK, TOK)
        mine_ref[i * TOK : (i + 1) * TOK] = held[pl.ds(at, TOK)]
        at = pl.multiple_of(i * 2 * TOK + (1 - core) * TOK, TOK)
        other_ref[i * TOK : (i + 1) * TOK] = held[pl.ds(at, TOK)]


def local_kernel(body, outs, scalars=(), scratch=(), flops=1 << 27, grant=16):
    vmem = pl.BlockSpec(memory_space=pltpu.VMEM)
    smem = pl.BlockSpec(memory_space=pltpu.SMEM)

    def call(*operands):
        given = (jnp.stack([s.astype(jnp.int32) for s in scalars]),) if scalars else ()
        return pl.pallas_call(
            body,
            out_shape=[jax.ShapeDtypeStruct(*o) for o in outs],
            in_specs=[smem] * len(given) + [vmem] * len(operands),
            out_specs=[vmem] * len(outs),
            scratch_shapes=list(scratch),
            compiler_params=pltpu.CompilerParams(vmem_limit_bytes=grant << 20),
            cost_estimate=pl.CostEstimate(
                flops=flops, bytes_accessed=2 << 20, transcendentals=1 << 18
            ),
        )(*given, *operands)

    return call


def state_call(keys, values, log_decay):
    rows = keys.shape[0]
    return local_kernel(
        state_kernel,
        [((2, MSG, HEAD_DIM), BF16), ((rows, HEAD_DIM), F32), ((16, rows), F32)],
        flops=1 << 28,
    )(keys, values, log_decay)


def within_call(queries, keys, values, col, row):
    return local_kernel(within_kernel, [(queries.shape, F32)], flops=1 << 29)(
        queries, keys, values, col, row
    )[0]


def fold_call(messages, place):
    return local_kernel(
        fold_kernel,
        [((2, MSG, HEAD_DIM), BF16), ((2, HEAD_DIM + 8, HEAD_DIM), F32)],
        scalars=(place,),
    )(*messages)


def mix_call(messages, before, queries, col, within, place, core):
    rows, cols = queries.shape
    return local_kernel(
        mix_kernel,
        [((rows // 2, cols), BF16)] * 2,
        scalars=(place, core),
        scratch=[pltpu.VMEM((rows, cols), BF16)],
    )(*messages, before, queries, col, within)


def attention(queries, keys, values, log_decay):
    message, col, row = state_call(keys, values, log_decay)
    messages = [message] + [shift(message, "y", d) for d in (1, 2, 3)]
    within = within_call(queries, keys, values, col, row)
    message, before = fold_call(messages, lax.axis_index("y"))
    messages = [message] + [shift(message, "x", d) for d in (1, 2, 3)]
    places = [lax.axis_index(a) for a in ("x", "c")]
    return mix_call(messages, before, queries, col, within, *places)


def arrange_kernel(a_ref, b_ref, c_ref, *outs):
    first = [(a_ref, 0), (b_ref, 0), (c_ref, 0), (b_ref, 1)]
    second = [(a_ref, 1), (b_ref, 2), (c_ref, 1), (b_ref, 3)]
    for dx in range(4):
        for dy in range(4):
            ref, at = first[dy]
            outs[dx][dy * 96 : dy * 96 + 48] = ref[at * 192 + dx * 48 : at * 192 + dx * 48 + 48]
            ref, at = second[dx]
            outs[dx][dy * 96 + 48 : dy * 96 + 96] = ref[
                at * 192 + dy * 48 : at * 192 + dy * 48 + 48
            ]


def arrange(a, b, c):
    units = a.shape[1]
    return pl.pallas_call(
        arrange_kernel,
        out_shape=[jax.ShapeDtypeStruct((384, units), BF16)] * 4,
        compiler_params=pltpu.CompilerParams(vmem_limit_bytes=6 << 20),
        cost_estimate=pl.CostEstimate(flops=0, bytes_accessed=2 << 20, transcendentals=0),
    )(a, b, c)


def beside_kernel(place_ref, p0, p1, p2, p3, out_ref):
    units = p0.shape[1]
    for d, piece in enumerate((p0, p1, p2, p3)):
        at = lax.rem(place_ref[0] + 4 - d, 4)
        out_ref[:, pl.ds(pl.multiple_of(at * units, 128), units)] = piece[...]


def down(pieces, weights, place):
    rows, units = pieces[0].shape
    beside = local_kernel(
        beside_kernel, [((rows, 4 * units), BF16)], scalars=(place,), flops=1 << 20, grant=6
    )(*pieces)[0]
    product = dot(beside, weights).astype(BF16)
    return [product[i * 96 : i * 96 + 96] for i in range(4)]


def refold_kernel(p0, p1, p2, p3, fold_ref, *outs):
    for half in range(2):
        at = slice(half * 48, half * 48 + 48)
        total = sum(p[at].astype(F32) for p in (p0, p1, p2, p3)).astype(BF16)
        rows = 0.0
        for i in range(QUARTERS):
            rows = rows + dot(fold_ref[i], total[:, i * QCOLS : (i + 1) * QCOLS])
        rows = rows.astype(BF16)
        row = 0
        for out in outs[:4] if half == 0 else outs[4:]:
            out[...] = rows[row : row + out.shape[0]]
            row += out.shape[0]


def refold(parts, fold):
    return pl.pallas_call(
        refold_kernel,
        out_shape=[jax.ShapeDtypeStruct((n, QCOLS), BF16) for n in (48, 48, 48, 48, 144, 48)],
        compiler_params=pltpu.CompilerParams(vmem_limit_bytes=12 << 20),
        cost_estimate=pl.CostEstimate(flops=2 << 27, bytes_accessed=3 << 20, transcendentals=0),
    )(*parts, fold)


def unfold_matrix():
    row = jnp.arange(48)
    place, core, slot = row // 12, (row // 6) % 2, row % 6
    quarter = jnp.arange(QUARTERS)[:, None]
    source = place * 48 + core * 24 + quarter * 6 + slot
    return (source[:, :, None] == jnp.arange(192)[None, None, :]).astype(BF16)


def shards(
    queries, keys, values, log_decay, residual, out_weight, router, w_gate, w_up, w_down, routes
):
    z, c = lax.axis_index("z"), lax.axis_index("c")
    x = lax.axis_index("x")
    down_all = lax.all_gather(w_down[0], "x", axis=0, tiled=True)
    weight_pair = jnp.concatenate([out_weight, swap(out_weight, "c")], axis=0)
    gate_up = jnp.concatenate([w_gate[0], w_up[0]], axis=1)

    ids = jnp.arange(16)
    carrier = c ^ (ids // 8)
    kind = ids % 8
    away = jnp.where(kind < 6, (1 - 2 * carrier) * (kind // 2 + 1), jnp.where(kind == 6, 4, 0))
    crossed = jnp.where(kind < 6, kind % 2, 0)
    relative = 2 * ((z + away + NZ) % NZ) + (carrier ^ crossed)
    named = (routes[:, :, None] == relative[None, None, :]).any(axis=1)
    member = named.astype(F32)
    earlier = (jnp.arange(TOK)[:, None] > jnp.arange(TOK)[None, :]).astype(F32)
    slot = jnp.dot(earlier, member).astype(jnp.int32)
    router_rel = dot(
        router, (ids[:, None] == relative[None, :]).astype(BF16)
    ).astype(BF16)
    chosen = named[:, :, None] & (slot[:, :, None] == jnp.arange(CAP)[None, None, :])
    chosen = chosen.reshape(TOK, NC, NZ, CAP).transpose(1, 2, 3, 0)
    same = jnp.eye(QUARTERS, dtype=jnp.bool_)
    dispatch = chosen[:, :, None, :, None, :] & same[None, None, :, None, :, None]
    dispatch = dispatch.reshape(NC, NZ * QUARTERS * CAP, QUARTERS * TOK)
    dispatch_bf = dispatch.astype(BF16)

    mine, theirs = attention(queries, keys, values, log_decay)
    both = jnp.concatenate([mine, swap(theirs, "c")], axis=1)
    projected = dot(both, weight_pair).astype(BF16).reshape(NZ, TOK, D)
    attn = lax.dynamic_index_in_dim(projected, z, 0, keepdims=False).astype(F32)
    parts = [
        shift(lax.dynamic_index_in_dim(projected, (z + d) % NZ, 0, keepdims=False), "z", d)
        for d in (1, 7, 2, 6, 3, 5, 4)
    ]
    for part in parts:
        attn = attn + part.astype(F32)
    hidden = residual.astype(F32) + attn
    normed = (hidden * lax.rsqrt(jnp.mean(hidden * hidden, axis=-1, keepdims=True) + 1e-06)).astype(
        BF16
    )
    logits = dot(normed, router_rel)
    picked = jax.nn.sigmoid(logits) * member
    gates = picked / jnp.sum(picked, axis=1, keepdims=True)

    folded = jnp.concatenate(
        [normed[:, i * QCOLS : (i + 1) * QCOLS] for i in range(QUARTERS)], axis=0
    )
    keep = dot(dispatch_bf[0], folded).astype(BF16).reshape(8, 24, QCOLS)
    got = swap(dot(dispatch_bf[1], folded).astype(BF16), "c").reshape(8, 24, QCOLS)
    out_rows = [
        jnp.concatenate([keep[2 * j], got[2 * j], keep[2 * j + 1], got[2 * j + 1]], axis=0)
        for j in range(3)
    ]
    opposite = jnp.concatenate([keep[6], got[6]], axis=0)
    stayed = jnp.concatenate([keep[7], got[7]], axis=0)
    opposite = part_ways(opposite, 4)
    arrived = [part_ways(out_rows[j], j + 1) for j in range(3)]
    opposite, *arrived = lax.optimization_barrier((opposite, *arrived))
    crossing = swap(jnp.concatenate([v[48:] for v in arrived], axis=0), "c")
    unfold = unfold_matrix()

    def unfolded(blocks):
        block = jnp.concatenate(blocks, axis=0)
        return jnp.concatenate(
            [dot(unfold[i], block).astype(BF16) for i in range(QUARTERS)], axis=1
        )

    first = unfolded([v[:48] for v in arrived] + [stayed])
    second = unfolded([crossing, opposite])
    rows_x, rows_y = lax.optimization_barrier(
        (jnp.concatenate(ahead(first, "x"), axis=0), jnp.concatenate(ahead(second, "y"), axis=0))
    )
    by_y, by_x = ahead_split(rows_x, "y"), ahead_split(rows_y, "x")

    def expert_hidden(blocks):
        product = dot(jnp.concatenate(blocks, axis=0), gate_up)
        gate_part, up_part = jnp.split(product, 2, axis=1)
        return (jax.nn.silu(gate_part) * up_part).astype(BF16)

    hidden_a = expert_hidden([by_y[0], by_x[0]])
    hidden_b = expert_hidden([by_y[1], by_y[3], by_x[1], by_x[3]])
    hidden_c = expert_hidden([by_y[2], by_x[2]])
    sends = arrange(hidden_a, hidden_b, hidden_c)
    pieces = [sends[0]] + [shift(sends[d], "x", d) for d in (1, 2, 3)]
    partial = down(pieces, down_all, x)
    parts = [partial[0]] + [shift(partial[d], "y", d) for d in (1, 2, 3)]
    own1, own2, own3, stayed, crossing, opposite = refold(parts, unfold.transpose(0, 2, 1))
    crossing = swap(crossing, "c")
    home = [
        part_ways(jnp.concatenate([own, crossing[48 * j : 48 * j + 48]], axis=0), j + 1, True)
        for j, own in enumerate((own1, own2, own3))
    ]
    opposite = part_ways(opposite, 4, True)
    kept = [v[at : at + 24] for v in home for at in (0, 48)] + [opposite[:24], stayed[:24]]
    given = [v[at : at + 24] for v in home for at in (24, 72)] + [opposite[24:], stayed[24:]]
    kept = jnp.concatenate(kept, axis=0)
    given = swap(jnp.concatenate(given, axis=0), "c")

    gates_rel = gates.reshape(TOK, NC, NZ).transpose(1, 2, 0)
    spread = jnp.broadcast_to(
        gates_rel[:, :, None, None, None, :], (NC, NZ, QUARTERS, CAP, QUARTERS, TOK)
    ).reshape(NC, NZ * QUARTERS * CAP, QUARTERS * TOK)
    weights = jnp.where(dispatch, spread, 0.0)
    combined = 0.0
    for rows, weight in ((kept, weights[0]), (given, weights[1])):
        for part in split_hi_lo(weight):
            combined = combined + lax.dot_general(
                part, rows, (((0,), (0,)), ((), ())), preferred_element_type=F32
            )
    combined = jnp.concatenate(
        [combined[i * TOK : (i + 1) * TOK] for i in range(QUARTERS)], axis=1
    )
    return (hidden + combined).astype(BF16)


def solution(mesh):
    grid = Mesh(mesh.devices.reshape(NX, NY, NZ, NC), ("x", "y", "z", "c"))
    seq, exp = ("x", "y"), ("z", "c")
    placed = (
        P(seq, exp),
        P(seq, exp),
        P(seq, exp),
        P(seq, exp),
        P(seq + exp, None),
        P(exp, None),
        P(),
        P(exp, None, seq),
        P(exp, None, seq),
        P(exp, seq, None),
        P(seq + exp, None),
    )
    return jax.shard_map(
        shards, mesh=grid, in_specs=placed, out_specs=P(seq + exp, None), check_vma=False
    )
```

```python
import jax
import jax.numpy as jnp
from jax import lax
from jax.experimental import pallas as pl
from jax.experimental.pallas import tpu as pltpu
from jax.sharding import Mesh, PartitionSpec as P

D = 3072
HEAD_DIM = 128
TOK = 32
CAP = 6
QUARTERS = 4
QCOLS = D // QUARTERS
NX, NY, NZ, NC = 4, 4, 8, 2
SIZES = {"x": NX, "y": NY, "z": NZ, "c": NC}
F32, BF16 = jnp.float32, jnp.bfloat16


def shift(v, axis, by):
    n = SIZES[axis]
    return lax.ppermute(v, axis, [(i, (i + by) % n) for i in range(n)])


def part_ways(v, by, back=False):
    pairs = []
    for z in range(NZ):
        for c in range(NC):
            there = (z + (1 - 2 * c) * by) % NZ
            pairs.append((z * NC + c, there * NC + c))
    if back:
        pairs = [(there, here) for here, there in pairs]
    return lax.ppermute(v, ("z", "c"), pairs)


def swap(v, axis):
    return lax.ppermute(v, axis, [(i, i ^ 1) for i in range(SIZES[axis])])


def ahead(v, axis):
    return [v, shift(v, axis, -1), shift(v, axis, 2), shift(v, axis, 1)]


def ahead_split(v, axis):
    up, down = shift(v, axis, -1), shift(v, axis, 1)
    half = v.shape[0] // 2
    far = jnp.concatenate([shift(up[:half], axis, -1), shift(down[half:], axis, 1)], axis=0)
    return [v, up, far, down]


def dot(a, b):
    return jnp.dot(a, b, preferred_element_type=F32)


def split_hi_lo(v):
    hi = v.astype(BF16)
    return hi, (v - hi.astype(F32)).astype(BF16)


MSG = HEAD_DIM + 16


def parts_of(v):
    hi, rest = split_hi_lo(v)
    mid = (v - hi.astype(F32)).astype(BF16)
    return hi, mid, (v - hi.astype(F32) - mid.astype(F32)).astype(BF16)


def message_rows(total):
    hi, lo = split_hi_lo(total)
    row = lax.broadcasted_iota(jnp.int32, (16, HEAD_DIM), 0)
    rows = jnp.where(row == 0, hi.astype(F32), jnp.where(row == 1, lo.astype(F32), 0.0))
    return rows.astype(BF16)


def state_kernel(k_ref, v_ref, decay_ref, message_ref, col_ref, row_ref):
    rows = k_ref.shape[0]
    lane = lax.broadcasted_iota(jnp.int32, (rows, HEAD_DIM), 1)
    decay = jnp.where(lane < 64, decay_ref[:, 0:1], decay_ref[:, 1:2])
    tri = (
        lax.broadcasted_iota(jnp.int32, (rows, rows), 0)
        >= lax.broadcasted_iota(jnp.int32, (rows, rows), 1)
    ).astype(F32).astype(BF16)
    col, row = 0.0, 0.0
    for part in parts_of(decay):
        col = col + dot(tri, part)
        row = row + lax.dot_general(
            part, tri, (((0,), (1,)), ((), ())), preferred_element_type=F32
        )
    col_ref[...] = col
    for h in range(2):
        row_ref[h * 8 : h * 8 + 8] = row[h * 64 : h * 64 + 8]
        cols = slice(h * HEAD_DIM, (h + 1) * HEAD_DIM)
        here = jnp.broadcast_to(col[:, h * 64 : h * 64 + 1], (rows, HEAD_DIM))
        tail = here[rows - 1 : rows]
        scaled = k_ref[:, cols].astype(F32) * jnp.exp(tail - here)
        state = 0.0
        for part in split_hi_lo(scaled):
            state = state + lax.dot_general(
                part, v_ref[:, cols], (((0,), (0,)), ((), ())), preferred_element_type=F32
            )
        message_ref[h, :HEAD_DIM] = state.astype(BF16)
        message_ref[h, HEAD_DIM:] = message_rows(tail)


def within_kernel(q_ref, k_ref, v_ref, col_ref, row_ref, out_ref):
    rows = q_ref.shape[0]
    step = 256
    for h in range(2):
        cols = slice(h * HEAD_DIM, (h + 1) * HEAD_DIM)
        for start in range(0, rows, step):
            stop = start + step
            scores = lax.dot_general(
                q_ref[start:stop, cols],
                k_ref[:stop, cols],
                (((1,), (1,)), ((), ())),
                preferred_element_type=F32,
            )
            apart = col_ref[start:stop, h * 64 : h * 64 + 1] - row_ref[h * 8 : h * 8 + 1, :stop]
            causal = start + lax.broadcasted_iota(
                jnp.int32, (step, stop), 0
            ) >= lax.broadcasted_iota(jnp.int32, (step, stop), 1)
            damped = scores * jnp.where(causal, jnp.exp(jnp.minimum(apart, 0.0)), 0.0)
            total = 0.0
            for part in split_hi_lo(damped):
                total = total + dot(part, v_ref[:stop, cols])
            out_ref[start:stop, cols] = total


def fold(messages, h, place):
    totals = [m[h, HEAD_DIM:].astype(F32) for m in messages]
    totals = [t[0:1] + t[1:2] for t in totals]
    states = [m[h, :HEAD_DIM].astype(F32) for m in messages]
    where = [lax.rem(place + 4 - d, 4) for d in range(4)]
    ordered = [sum(jnp.where(where[d] == j, totals[d], 0.0) for d in range(4)) for j in range(4)]
    before, everything = 0.0, 0.0
    for d in range(4):
        till_here = sum(
            jnp.where((j > where[d]) & (j < place), ordered[j], 0.0) for j in range(4)
        )
        till_end = sum(jnp.where(j > where[d], ordered[j], 0.0) for j in range(4))
        before = before + jnp.where(where[d] < place, jnp.exp(till_here), 0.0) * states[d]
        everything = everything + jnp.exp(till_end) * states[d]
    total_before = sum(jnp.where(j < place, ordered[j], 0.0) for j in range(4))
    return before, total_before, everything, sum(ordered)


def fold_kernel(place_ref, m0, m1, m2, m3, message_ref, before_ref):
    for h in range(2):
        before, total_before, everything, total = fold((m0, m1, m2, m3), h, place_ref[0])
        before_ref[h, :HEAD_DIM] = before
        before_ref[h, HEAD_DIM:] = jnp.broadcast_to(jnp.exp(total_before), (8, HEAD_DIM))
        message_ref[h, :HEAD_DIM] = everything.astype(BF16)
        message_ref[h, HEAD_DIM:] = message_rows(total)


def mix_kernel(
    place_ref, m0, m1, m2, m3, before_ref, q_ref, col_ref, within_ref, mine_ref, other_ref, held
):
    for h in range(2):
        cols = slice(h * HEAD_DIM, (h + 1) * HEAD_DIM)
        earlier, _, _, _ = fold((m0, m1, m2, m3), h, place_ref[0])
        state = before_ref[h, :HEAD_DIM] + before_ref[h, HEAD_DIM : HEAD_DIM + 1] * earlier
        carried = 0.0
        for part in split_hi_lo(state):
            carried = carried + dot(q_ref[:, cols], part)
        mixed = within_ref[:, cols] + jnp.exp(col_ref[:, h * 64 : h * 64 + 1]) * carried
        scale = lax.rsqrt(jnp.mean(mixed * mixed, axis=-1, keepdims=True) + 1e-06)
        held[:, cols] = (mixed * scale).astype(BF16)
    core = place_ref[1]
    for i in range(NZ):
        at = pl.multiple_of(i * 2 * TOK + core * TOK, TOK)
        mine_ref[i * TOK : (i + 1) * TOK] = held[pl.ds(at, TOK)]
        at = pl.multiple_of(i * 2 * TOK + (1 - core) * TOK, TOK)
        other_ref[i * TOK : (i + 1) * TOK] = held[pl.ds(at, TOK)]


def local_kernel(body, outs, scalars=(), scratch=(), flops=1 << 27, grant=16):
    vmem = pl.BlockSpec(memory_space=pltpu.VMEM)
    smem = pl.BlockSpec(memory_space=pltpu.SMEM)

    def call(*operands):
        given = (jnp.stack([s.astype(jnp.int32) for s in scalars]),) if scalars else ()
        return pl.pallas_call(
            body,
            out_shape=[jax.ShapeDtypeStruct(*o) for o in outs],
            in_specs=[smem] * len(given) + [vmem] * len(operands),
            out_specs=[vmem] * len(outs),
            scratch_shapes=list(scratch),
            compiler_params=pltpu.CompilerParams(vmem_limit_bytes=grant << 20),
            cost_estimate=pl.CostEstimate(
                flops=flops, bytes_accessed=2 << 20, transcendentals=1 << 18
            ),
        )(*given, *operands)

    return call


def state_call(keys, values, log_decay):
    rows = keys.shape[0]
    return local_kernel(
        state_kernel,
        [((2, MSG, HEAD_DIM), BF16), ((rows, HEAD_DIM), F32), ((16, rows), F32)],
        flops=1 << 28,
    )(keys, values, log_decay)


def within_call(queries, keys, values, col, row):
    return local_kernel(within_kernel, [(queries.shape, F32)], flops=1 << 29)(
        queries, keys, values, col, row
    )[0]


def fold_call(messages, place):
    return local_kernel(
        fold_kernel,
        [((2, MSG, HEAD_DIM), BF16), ((2, HEAD_DIM + 8, HEAD_DIM), F32)],
        scalars=(place,),
    )(*messages)


def mix_call(messages, before, queries, col, within, place, core):
    rows, cols = queries.shape
    return local_kernel(
        mix_kernel,
        [((rows // 2, cols), BF16)] * 2,
        scalars=(place, core),
        scratch=[pltpu.VMEM((rows, cols), BF16)],
    )(*messages, before, queries, col, within)


def attention(queries, keys, values, log_decay):
    message, col, row = state_call(keys, values, log_decay)
    messages = [message] + [shift(message, "y", d) for d in (1, 2, 3)]
    within = within_call(queries, keys, values, col, row)
    message, before = fold_call(messages, lax.axis_index("y"))
    messages = [message] + [shift(message, "x", d) for d in (1, 2, 3)]
    places = [lax.axis_index(a) for a in ("x", "c")]
    return mix_call(messages, before, queries, col, within, *places)


def arrange_kernel(a_ref, b_ref, c_ref, *outs):
    first = [(a_ref, 0), (b_ref, 0), (c_ref, 0), (b_ref, 1)]
    second = [(a_ref, 1), (b_ref, 2), (c_ref, 1), (b_ref, 3)]
    for dx in range(4):
        for dy in range(4):
            ref, at = first[dy]
            outs[dx][dy * 96 : dy * 96 + 48] = ref[at * 192 + dx * 48 : at * 192 + dx * 48 + 48]
            ref, at = second[dx]
            outs[dx][dy * 96 + 48 : dy * 96 + 96] = ref[
                at * 192 + dy * 48 : at * 192 + dy * 48 + 48
            ]


def arrange(a, b, c):
    units = a.shape[1]
    return pl.pallas_call(
        arrange_kernel,
        out_shape=[jax.ShapeDtypeStruct((384, units), BF16)] * 4,
        compiler_params=pltpu.CompilerParams(vmem_limit_bytes=6 << 20),
        cost_estimate=pl.CostEstimate(flops=0, bytes_accessed=2 << 20, transcendentals=0),
    )(a, b, c)


def beside_kernel(place_ref, p0, p1, p2, p3, out_ref):
    units = p0.shape[1]
    for d, piece in enumerate((p0, p1, p2, p3)):
        at = lax.rem(place_ref[0] + 4 - d, 4)
        out_ref[:, pl.ds(pl.multiple_of(at * units, 128), units)] = piece[...]


def down(pieces, weights, place):
    rows, units = pieces[0].shape
    beside = local_kernel(
        beside_kernel, [((rows, 4 * units), BF16)], scalars=(place,), flops=1 << 20, grant=6
    )(*pieces)[0]
    leaving = dot(beside[96:], weights).astype(BF16)
    own = dot(beside[:96], weights).astype(BF16)
    return [own] + [leaving[i * 96 : i * 96 + 96] for i in range(3)]


def refold_kernel(p0, p1, p2, fold_ref, *outs):
    for half in range(2):
        at = slice(half * 48, half * 48 + 48)
        total = sum(p[at].astype(F32) for p in (p0, p1, p2)).astype(BF16)
        rows = 0.0
        for i in range(QUARTERS):
            rows = rows + dot(fold_ref[i], total[:, i * QCOLS : (i + 1) * QCOLS])
        rows = rows.astype(BF16)
        row = 0
        for out in outs[:4] if half == 0 else outs[4:]:
            out[...] = rows[row : row + out.shape[0]]
            row += out.shape[0]


def refold(parts, fold):
    return pl.pallas_call(
        refold_kernel,
        out_shape=[jax.ShapeDtypeStruct((n, QCOLS), BF16) for n in (48, 48, 48, 48, 144, 48)],
        compiler_params=pltpu.CompilerParams(vmem_limit_bytes=12 << 20),
        cost_estimate=pl.CostEstimate(flops=2 << 27, bytes_accessed=3 << 20, transcendentals=0),
    )(*parts, fold)


def unfold_matrix():
    row = jnp.arange(48)
    place, core, slot = row // 12, (row // 6) % 2, row % 6
    quarter = jnp.arange(QUARTERS)[:, None]
    source = place * 48 + core * 24 + quarter * 6 + slot
    return (source[:, :, None] == jnp.arange(192)[None, None, :]).astype(BF16)


def shards(
    queries, keys, values, log_decay, residual, out_weight, router, w_gate, w_up, w_down, routes
):
    z, c = lax.axis_index("z"), lax.axis_index("c")
    x = lax.axis_index("x")
    down_all = lax.all_gather(w_down[0], "x", axis=0, tiled=True)
    weight_pair = jnp.concatenate([out_weight, swap(out_weight, "c")], axis=0)
    gate_up = jnp.concatenate([w_gate[0], w_up[0]], axis=1)

    ids = jnp.arange(16)
    carrier = c ^ (ids // 8)
    kind = ids % 8
    away = jnp.where(kind < 6, (1 - 2 * carrier) * (kind // 2 + 1), jnp.where(kind == 6, 4, 0))
    crossed = jnp.where(kind < 6, kind % 2, 0)
    relative = 2 * ((z + away + NZ) % NZ) + (carrier ^ crossed)
    named = (routes[:, :, None] == relative[None, None, :]).any(axis=1)
    member = named.astype(F32)
    earlier = (jnp.arange(TOK)[:, None] > jnp.arange(TOK)[None, :]).astype(F32)
    slot = jnp.dot(earlier, member).astype(jnp.int32)
    router_rel = dot(
        router, (ids[:, None] == relative[None, :]).astype(BF16)
    ).astype(BF16)
    chosen = named[:, :, None] & (slot[:, :, None] == jnp.arange(CAP)[None, None, :])
    chosen = chosen.reshape(TOK, NC, NZ, CAP).transpose(1, 2, 3, 0)
    same = jnp.eye(QUARTERS, dtype=jnp.bool_)
    dispatch = chosen[:, :, None, :, None, :] & same[None, None, :, None, :, None]
    dispatch = dispatch.reshape(NC, NZ * QUARTERS * CAP, QUARTERS * TOK)
    dispatch_bf = dispatch.astype(BF16)

    mine, theirs = attention(queries, keys, values, log_decay)
    both = jnp.concatenate([mine, swap(theirs, "c")], axis=1)
    projected = dot(both, weight_pair).astype(BF16).reshape(NZ, TOK, D)
    attn = lax.dynamic_index_in_dim(projected, z, 0, keepdims=False).astype(F32)
    parts = [
        shift(lax.dynamic_index_in_dim(projected, (z + d) % NZ, 0, keepdims=False), "z", d)
        for d in (1, 7, 2, 6, 3, 5, 4)
    ]
    for part in parts:
        attn = attn + part.astype(F32)
    hidden = residual.astype(F32) + attn
    normed = (hidden * lax.rsqrt(jnp.mean(hidden * hidden, axis=-1, keepdims=True) + 1e-06)).astype(
        BF16
    )
    logits = dot(normed, router_rel)
    picked = jax.nn.sigmoid(logits) * member
    gates = picked / jnp.sum(picked, axis=1, keepdims=True)

    folded = jnp.concatenate(
        [normed[:, i * QCOLS : (i + 1) * QCOLS] for i in range(QUARTERS)], axis=0
    )
    keep = dot(dispatch_bf[0], folded).astype(BF16).reshape(8, 24, QCOLS)
    got = swap(dot(dispatch_bf[1], folded).astype(BF16), "c").reshape(8, 24, QCOLS)
    out_rows = [
        jnp.concatenate([keep[2 * j], got[2 * j], keep[2 * j + 1], got[2 * j + 1]], axis=0)
        for j in range(3)
    ]
    opposite = jnp.concatenate([keep[6], got[6]], axis=0)
    stayed = jnp.concatenate([keep[7], got[7]], axis=0)
    opposite = part_ways(opposite, 4)
    arrived = [part_ways(out_rows[j], j + 1) for j in range(3)]
    opposite, *arrived = lax.optimization_barrier((opposite, *arrived))
    crossing = swap(jnp.concatenate([v[48:] for v in arrived], axis=0), "c")
    unfold = unfold_matrix()

    def unfolded(blocks):
        block = jnp.concatenate(blocks, axis=0)
        return jnp.concatenate(
            [dot(unfold[i], block).astype(BF16) for i in range(QUARTERS)], axis=1
        )

    first = unfolded([v[:48] for v in arrived] + [stayed])
    second = unfolded([crossing, opposite])
    rows_x, rows_y, down_all = lax.optimization_barrier(
        (
            jnp.concatenate(ahead(first, "x"), axis=0),
            jnp.concatenate(ahead(second, "y"), axis=0),
            down_all,
        )
    )
    by_y, by_x = ahead_split(rows_x, "y"), ahead_split(rows_y, "x")

    def expert_hidden(blocks):
        product = dot(jnp.concatenate(blocks, axis=0), gate_up)
        gate_part, up_part = jnp.split(product, 2, axis=1)
        return (jax.nn.silu(gate_part) * up_part).astype(BF16)

    hidden_a = expert_hidden([by_y[0], by_x[0]])
    hidden_b = expert_hidden([by_y[1], by_y[3], by_x[1], by_x[3]])
    hidden_c = expert_hidden([by_y[2], by_x[2]])
    sends = arrange(hidden_a, hidden_b, hidden_c)
    pieces = [sends[0]] + [shift(sends[d], "x", d) for d in (1, 2, 3)]
    own, ahead_one, far, behind_one = down(pieces, down_all, x)
    via_ahead, via_behind = shift(far[:48], "y", 1), shift(far[48:], "y", -1)

    def added(a, b):
        return (a.astype(F32) + b.astype(F32)).astype(BF16)

    ahead_one = jnp.concatenate([added(ahead_one[:48], via_ahead), ahead_one[48:]], axis=0)
    behind_one = jnp.concatenate([behind_one[:48], added(behind_one[48:], via_behind)], axis=0)
    parts = [own, shift(ahead_one, "y", 1), shift(behind_one, "y", -1)]
    own1, own2, own3, stayed, crossing, opposite = refold(parts, unfold.transpose(0, 2, 1))
    crossing = swap(crossing, "c")
    home = [
        part_ways(jnp.concatenate([own, crossing[48 * j : 48 * j + 48]], axis=0), j + 1, True)
        for j, own in enumerate((own1, own2, own3))
    ]
    opposite = part_ways(opposite, 4, True)
    kept = [v[at : at + 24] for v in home for at in (0, 48)] + [opposite[:24], stayed[:24]]
    given = [v[at : at + 24] for v in home for at in (24, 72)] + [opposite[24:], stayed[24:]]
    kept = jnp.concatenate(kept, axis=0)
    given = swap(jnp.concatenate(given, axis=0), "c")

    gates_rel = gates.reshape(TOK, NC, NZ).transpose(1, 2, 0)
    spread = jnp.broadcast_to(
        gates_rel[:, :, None, None, None, :], (NC, NZ, QUARTERS, CAP, QUARTERS, TOK)
    ).reshape(NC, NZ * QUARTERS * CAP, QUARTERS * TOK)
    weights = jnp.where(dispatch, spread, 0.0)
    combined = 0.0
    for rows, weight in ((kept, weights[0]), (given, weights[1])):
        for part in split_hi_lo(weight):
            combined = combined + lax.dot_general(
                part, rows, (((0,), (0,)), ((), ())), preferred_element_type=F32
            )
    combined = jnp.concatenate(
        [combined[i * TOK : (i + 1) * TOK] for i in range(QUARTERS)], axis=1
    )
    return (hidden + combined).astype(BF16)


def solution(mesh):
    grid = Mesh(mesh.devices.reshape(NX, NY, NZ, NC), ("x", "y", "z", "c"))
    seq, exp = ("x", "y"), ("z", "c")
    placed = (
        P(seq, exp),
        P(seq, exp),
        P(seq, exp),
        P(seq, exp),
        P(seq + exp, None),
        P(exp, None),
        P(),
        P(exp, None, seq),
        P(exp, None, seq),
        P(exp, seq, None),
        P(seq + exp, None),
    )
    return jax.shard_map(
        shards, mesh=grid, in_specs=placed, out_specs=P(seq + exp, None), check_vma=False
    )
```

```python
import jax
import jax.numpy as jnp
from jax import lax
from jax.experimental import pallas as pl
from jax.experimental.pallas import tpu as pltpu
from jax.sharding import Mesh, PartitionSpec as P

D = 3072
HEAD_DIM = 128
TOK = 32
CAP = 6
QUARTERS = 4
QCOLS = D // QUARTERS
NX, NY, NZ, NC = 4, 4, 8, 2
SIZES = {"x": NX, "y": NY, "z": NZ, "c": NC}
F32, BF16 = jnp.float32, jnp.bfloat16


def shift(v, axis, by):
    n = SIZES[axis]
    return lax.ppermute(v, axis, [(i, (i + by) % n) for i in range(n)])


def part_ways(v, by, back=False):
    pairs = []
    for z in range(NZ):
        for c in range(NC):
            there = (z + (1 - 2 * c) * by) % NZ
            pairs.append((z * NC + c, there * NC + c))
    if back:
        pairs = [(there, here) for here, there in pairs]
    return lax.ppermute(v, ("z", "c"), pairs)


def swap(v, axis):
    return lax.ppermute(v, axis, [(i, i ^ 1) for i in range(SIZES[axis])])


def ahead(v, axis):
    return [v, shift(v, axis, -1), shift(v, axis, 2), shift(v, axis, 1)]


def ahead_split(v, axis):
    up, down = shift(v, axis, -1), shift(v, axis, 1)
    half = v.shape[0] // 2
    far = jnp.concatenate([shift(up[:half], axis, -1), shift(down[half:], axis, 1)], axis=0)
    return [v, up, far, down]


def dot(a, b):
    return jnp.dot(a, b, preferred_element_type=F32)


def added(a, b):
    return (a.astype(F32) + b.astype(F32)).astype(BF16)


def split_hi_lo(v):
    hi = v.astype(BF16)
    return hi, (v - hi.astype(F32)).astype(BF16)


MSG = HEAD_DIM + 16


def parts_of(v):
    hi, rest = split_hi_lo(v)
    mid = (v - hi.astype(F32)).astype(BF16)
    return hi, mid, (v - hi.astype(F32) - mid.astype(F32)).astype(BF16)


def message_rows(total):
    hi, lo = split_hi_lo(total)
    row = lax.broadcasted_iota(jnp.int32, (16, HEAD_DIM), 0)
    rows = jnp.where(row == 0, hi.astype(F32), jnp.where(row == 1, lo.astype(F32), 0.0))
    return rows.astype(BF16)


def state_kernel(k_ref, v_ref, decay_ref, message_ref, col_ref, row_ref):
    rows = k_ref.shape[0]
    lane = lax.broadcasted_iota(jnp.int32, (rows, HEAD_DIM), 1)
    decay = jnp.where(lane < 64, decay_ref[:, 0:1], decay_ref[:, 1:2])
    tri = (
        lax.broadcasted_iota(jnp.int32, (rows, rows), 0)
        >= lax.broadcasted_iota(jnp.int32, (rows, rows), 1)
    ).astype(F32).astype(BF16)
    col, row = 0.0, 0.0
    for part in parts_of(decay):
        col = col + dot(tri, part)
        row = row + lax.dot_general(
            part, tri, (((0,), (1,)), ((), ())), preferred_element_type=F32
        )
    col_ref[...] = col
    for h in range(2):
        row_ref[h * 8 : h * 8 + 8] = row[h * 64 : h * 64 + 8]
        cols = slice(h * HEAD_DIM, (h + 1) * HEAD_DIM)
        here = jnp.broadcast_to(col[:, h * 64 : h * 64 + 1], (rows, HEAD_DIM))
        tail = here[rows - 1 : rows]
        scaled = k_ref[:, cols].astype(F32) * jnp.exp(tail - here)
        state = 0.0
        for part in split_hi_lo(scaled):
            state = state + lax.dot_general(
                part, v_ref[:, cols], (((0,), (0,)), ((), ())), preferred_element_type=F32
            )
        message_ref[h, :HEAD_DIM] = state.astype(BF16)
        message_ref[h, HEAD_DIM:] = message_rows(tail)


def within_kernel(q_ref, k_ref, v_ref, col_ref, row_ref, out_ref):
    rows = q_ref.shape[0]
    step = 256
    for h in range(2):
        cols = slice(h * HEAD_DIM, (h + 1) * HEAD_DIM)
        for start in range(0, rows, step):
            stop = start + step
            scores = lax.dot_general(
                q_ref[start:stop, cols],
                k_ref[:stop, cols],
                (((1,), (1,)), ((), ())),
                preferred_element_type=F32,
            )
            apart = col_ref[start:stop, h * 64 : h * 64 + 1] - row_ref[h * 8 : h * 8 + 1, :stop]
            causal = start + lax.broadcasted_iota(
                jnp.int32, (step, stop), 0
            ) >= lax.broadcasted_iota(jnp.int32, (step, stop), 1)
            damped = scores * jnp.where(causal, jnp.exp(jnp.minimum(apart, 0.0)), 0.0)
            total = 0.0
            for part in split_hi_lo(damped):
                total = total + dot(part, v_ref[:stop, cols])
            out_ref[start:stop, cols] = total


def fold(messages, h, place):
    totals = [m[h, HEAD_DIM:].astype(F32) for m in messages]
    totals = [t[0:1] + t[1:2] for t in totals]
    states = [m[h, :HEAD_DIM].astype(F32) for m in messages]
    where = [lax.rem(place + 4 - d, 4) for d in range(4)]
    ordered = [sum(jnp.where(where[d] == j, totals[d], 0.0) for d in range(4)) for j in range(4)]
    before, everything = 0.0, 0.0
    for d in range(4):
        till_here = sum(
            jnp.where((j > where[d]) & (j < place), ordered[j], 0.0) for j in range(4)
        )
        till_end = sum(jnp.where(j > where[d], ordered[j], 0.0) for j in range(4))
        before = before + jnp.where(where[d] < place, jnp.exp(till_here), 0.0) * states[d]
        everything = everything + jnp.exp(till_end) * states[d]
    total_before = sum(jnp.where(j < place, ordered[j], 0.0) for j in range(4))
    return before, total_before, everything, sum(ordered)


def fold_kernel(place_ref, m0, m1, m2, m3, message_ref, before_ref):
    for h in range(2):
        before, total_before, everything, total = fold((m0, m1, m2, m3), h, place_ref[0])
        before_ref[h, :HEAD_DIM] = before
        before_ref[h, HEAD_DIM:] = jnp.broadcast_to(jnp.exp(total_before), (8, HEAD_DIM))
        message_ref[h, :HEAD_DIM] = everything.astype(BF16)
        message_ref[h, HEAD_DIM:] = message_rows(total)


def mix_kernel(
    place_ref, m0, m1, m2, m3, before_ref, q_ref, col_ref, within_ref, mine_ref, other_ref, held
):
    for h in range(2):
        cols = slice(h * HEAD_DIM, (h + 1) * HEAD_DIM)
        earlier, _, _, _ = fold((m0, m1, m2, m3), h, place_ref[0])
        state = before_ref[h, :HEAD_DIM] + before_ref[h, HEAD_DIM : HEAD_DIM + 1] * earlier
        carried = 0.0
        for part in split_hi_lo(state):
            carried = carried + dot(q_ref[:, cols], part)
        mixed = within_ref[:, cols] + jnp.exp(col_ref[:, h * 64 : h * 64 + 1]) * carried
        scale = lax.rsqrt(jnp.mean(mixed * mixed, axis=-1, keepdims=True) + 1e-06)
        held[:, cols] = (mixed * scale).astype(BF16)
    core = place_ref[1]
    for i in range(NZ):
        at = pl.multiple_of(i * 2 * TOK + core * TOK, TOK)
        mine_ref[i * TOK : (i + 1) * TOK] = held[pl.ds(at, TOK)]
        at = pl.multiple_of(i * 2 * TOK + (1 - core) * TOK, TOK)
        other_ref[i * TOK : (i + 1) * TOK] = held[pl.ds(at, TOK)]


def local_kernel(body, outs, scalars=(), scratch=(), flops=1 << 27, grant=16):
    vmem = pl.BlockSpec(memory_space=pltpu.VMEM)
    smem = pl.BlockSpec(memory_space=pltpu.SMEM)

    def call(*operands):
        given = (jnp.stack([s.astype(jnp.int32) for s in scalars]),) if scalars else ()
        return pl.pallas_call(
            body,
            out_shape=[jax.ShapeDtypeStruct(*o) for o in outs],
            in_specs=[smem] * len(given) + [vmem] * len(operands),
            out_specs=[vmem] * len(outs),
            scratch_shapes=list(scratch),
            compiler_params=pltpu.CompilerParams(vmem_limit_bytes=grant << 20),
            cost_estimate=pl.CostEstimate(
                flops=flops, bytes_accessed=2 << 20, transcendentals=1 << 18
            ),
        )(*given, *operands)

    return call


def state_call(keys, values, log_decay):
    rows = keys.shape[0]
    return local_kernel(
        state_kernel,
        [((2, MSG, HEAD_DIM), BF16), ((rows, HEAD_DIM), F32), ((16, rows), F32)],
        flops=1 << 28,
    )(keys, values, log_decay)


def within_call(queries, keys, values, col, row):
    return local_kernel(within_kernel, [(queries.shape, F32)], flops=1 << 29)(
        queries, keys, values, col, row
    )[0]


def fold_call(messages, place):
    return local_kernel(
        fold_kernel,
        [((2, MSG, HEAD_DIM), BF16), ((2, HEAD_DIM + 8, HEAD_DIM), F32)],
        scalars=(place,),
    )(*messages)


def mix_call(messages, before, queries, col, within, place, core):
    rows, cols = queries.shape
    return local_kernel(
        mix_kernel,
        [((rows // 2, cols), BF16)] * 2,
        scalars=(place, core),
        scratch=[pltpu.VMEM((rows, cols), BF16)],
    )(*messages, before, queries, col, within)


def attention(queries, keys, values, log_decay):
    message, col, row = state_call(keys, values, log_decay)
    messages = [message] + [shift(message, "y", d) for d in (1, 2, 3)]
    within = within_call(queries, keys, values, col, row)
    message, before = fold_call(messages, lax.axis_index("y"))
    messages = [message] + [shift(message, "x", d) for d in (1, 2, 3)]
    places = [lax.axis_index(a) for a in ("x", "c")]
    return mix_call(messages, before, queries, col, within, *places)


def arrange_kernel(a_ref, b_ref, c_ref, *outs):
    first = [(a_ref, 0), (b_ref, 0), (c_ref, 0), (b_ref, 1)]
    second = [(a_ref, 1), (b_ref, 2), (c_ref, 1), (b_ref, 3)]
    for dx in range(4):
        for dy in range(4):
            ref, at = first[dy]
            outs[dx][dy * 96 : dy * 96 + 48] = ref[at * 192 + dx * 48 : at * 192 + dx * 48 + 48]
            ref, at = second[dx]
            outs[dx][dy * 96 + 48 : dy * 96 + 96] = ref[
                at * 192 + dy * 48 : at * 192 + dy * 48 + 48
            ]


def arrange(a, b, c):
    units = a.shape[1]
    return pl.pallas_call(
        arrange_kernel,
        out_shape=[jax.ShapeDtypeStruct((384, units), BF16)] * 4,
        compiler_params=pltpu.CompilerParams(vmem_limit_bytes=6 << 20),
        cost_estimate=pl.CostEstimate(flops=0, bytes_accessed=2 << 20, transcendentals=0),
    )(a, b, c)


def beside_kernel(place_ref, p0, p1, p2, p3, out_ref):
    units = p0.shape[1]
    for d, piece in enumerate((p0, p1, p2, p3)):
        at = lax.rem(place_ref[0] + 4 - d, 4)
        out_ref[:, pl.ds(pl.multiple_of(at * units, 128), units)] = piece[...]


def down(pieces, weights, place):
    rows, units = pieces[0].shape
    beside = local_kernel(
        beside_kernel, [((rows, 4 * units), BF16)], scalars=(place,), flops=1 << 20, grant=6
    )(*pieces)[0]
    leaving = dot(beside[96:], weights).astype(BF16)
    own = dot(beside[:96], weights).astype(BF16)
    return [own] + [leaving[i * 96 : i * 96 + 96] for i in range(3)]


def refold_kernel(p0, p1, p2, fold_ref, *outs):
    for half in range(2):
        at = slice(half * 48, half * 48 + 48)
        total = sum(p[at].astype(F32) for p in (p0, p1, p2)).astype(BF16)
        rows = 0.0
        for i in range(QUARTERS):
            rows = rows + dot(fold_ref[i], total[:, i * QCOLS : (i + 1) * QCOLS])
        rows = rows.astype(BF16)
        row = 0
        for out in outs[:4] if half == 0 else outs[4:]:
            out[...] = rows[row : row + out.shape[0]]
            row += out.shape[0]


def refold(parts, fold):
    return pl.pallas_call(
        refold_kernel,
        out_shape=[jax.ShapeDtypeStruct((n, QCOLS), BF16) for n in (48, 48, 48, 48, 144, 48)],
        compiler_params=pltpu.CompilerParams(vmem_limit_bytes=12 << 20),
        cost_estimate=pl.CostEstimate(flops=2 << 27, bytes_accessed=3 << 20, transcendentals=0),
    )(*parts, fold)


def unfold_matrix():
    row = jnp.arange(48)
    place, core, slot = row // 12, (row // 6) % 2, row % 6
    quarter = jnp.arange(QUARTERS)[:, None]
    source = place * 48 + core * 24 + quarter * 6 + slot
    return (source[:, :, None] == jnp.arange(192)[None, None, :]).astype(BF16)


def shards(
    queries, keys, values, log_decay, residual, out_weight, router, w_gate, w_up, w_down, routes
):
    z, c = lax.axis_index("z"), lax.axis_index("c")
    x = lax.axis_index("x")
    down_all = lax.all_gather(w_down[0], "x", axis=0, tiled=True)
    weight_pair = jnp.concatenate([out_weight, swap(out_weight, "c")], axis=0)
    gate_up = jnp.concatenate([w_gate[0], w_up[0]], axis=1)

    ids = jnp.arange(16)
    carrier = c ^ (ids // 8)
    kind = ids % 8
    away = jnp.where(kind < 6, (1 - 2 * carrier) * (kind // 2 + 1), jnp.where(kind == 6, 4, 0))
    crossed = jnp.where(kind < 6, kind % 2, 0)
    relative = 2 * ((z + away + NZ) % NZ) + (carrier ^ crossed)
    named = (routes[:, :, None] == relative[None, None, :]).any(axis=1)
    member = named.astype(F32)
    earlier = (jnp.arange(TOK)[:, None] > jnp.arange(TOK)[None, :]).astype(F32)
    slot = jnp.dot(earlier, member).astype(jnp.int32)
    router_rel = dot(
        router, (ids[:, None] == relative[None, :]).astype(BF16)
    ).astype(BF16)
    chosen = named[:, :, None] & (slot[:, :, None] == jnp.arange(CAP)[None, None, :])
    chosen = chosen.reshape(TOK, NC, NZ, CAP).transpose(1, 2, 3, 0)
    same = jnp.eye(QUARTERS, dtype=jnp.bool_)
    dispatch = chosen[:, :, None, :, None, :] & same[None, None, :, None, :, None]
    dispatch = dispatch.reshape(NC, NZ * QUARTERS * CAP, QUARTERS * TOK)
    dispatch_bf = dispatch.astype(BF16)

    mine, theirs = attention(queries, keys, values, log_decay)
    both = jnp.concatenate([mine, swap(theirs, "c")], axis=1)
    projected = dot(both, weight_pair).astype(BF16).reshape(NZ, TOK, D)

    def block(d):
        return lax.dynamic_index_in_dim(projected, (z + d) % NZ, 0, keepdims=False)

    half = TOK // 2
    from_below = shift(jnp.concatenate([block(2), block(4)[:half]], axis=0), "z", 1)
    from_above = shift(jnp.concatenate([block(6), block(4)[half:]], axis=0), "z", -1)
    three_up, three_down = block(3), block(5)
    sums = [
        (3, jnp.concatenate([added(three_up[:half], from_below[TOK:]), three_up[half:]], axis=0)),
        (5, jnp.concatenate([three_down[:half], added(three_down[half:], from_above[TOK:])], axis=0)),
        (1, added(block(1), from_below[:TOK])),
        (7, added(block(7), from_above[:TOK])),
    ]
    attn = block(0).astype(F32)
    for d, total in sums:
        attn = attn + shift(total, "z", d).astype(F32)
    hidden = residual.astype(F32) + attn
    normed = (hidden * lax.rsqrt(jnp.mean(hidden * hidden, axis=-1, keepdims=True) + 1e-06)).astype(
        BF16
    )
    logits = dot(normed, router_rel)
    picked = jax.nn.sigmoid(logits) * member
    gates = picked / jnp.sum(picked, axis=1, keepdims=True)

    folded = jnp.concatenate(
        [normed[:, i * QCOLS : (i + 1) * QCOLS] for i in range(QUARTERS)], axis=0
    )
    keep = dot(dispatch_bf[0], folded).astype(BF16).reshape(8, 24, QCOLS)
    got = swap(dot(dispatch_bf[1], folded).astype(BF16), "c").reshape(8, 24, QCOLS)
    out_rows = [
        jnp.concatenate([keep[2 * j], got[2 * j], keep[2 * j + 1], got[2 * j + 1]], axis=0)
        for j in range(3)
    ]
    opposite = jnp.concatenate([keep[6], got[6]], axis=0)
    stayed = jnp.concatenate([keep[7], got[7]], axis=0)
    opposite = part_ways(opposite, 4)
    arrived = [part_ways(out_rows[j], j + 1) for j in range(3)]
    opposite, *arrived = lax.optimization_barrier((opposite, *arrived))
    crossing = swap(jnp.concatenate([v[48:] for v in arrived], axis=0), "c")
    unfold = unfold_matrix()

    def unfolded(blocks):
        block = jnp.concatenate(blocks, axis=0)
        return jnp.concatenate(
            [dot(unfold[i], block).astype(BF16) for i in range(QUARTERS)], axis=1
        )

    first = unfolded([v[:48] for v in arrived] + [stayed])
    second = unfolded([crossing, opposite])
    rows_x, rows_y, down_all = lax.optimization_barrier(
        (
            jnp.concatenate(ahead(first, "x"), axis=0),
            jnp.concatenate(ahead(second, "y"), axis=0),
            down_all,
        )
    )
    by_y, by_x = ahead_split(rows_x, "y"), ahead_split(rows_y, "x")

    def expert_hidden(blocks):
        product = dot(jnp.concatenate(blocks, axis=0), gate_up)
        gate_part, up_part = jnp.split(product, 2, axis=1)
        return (jax.nn.silu(gate_part) * up_part).astype(BF16)

    hidden_a = expert_hidden([by_y[0], by_x[0]])
    hidden_b = expert_hidden([by_y[1], by_y[3], by_x[1], by_x[3]])
    hidden_c = expert_hidden([by_y[2], by_x[2]])
    sends = arrange(hidden_a, hidden_b, hidden_c)
    pieces = [sends[0]] + [shift(sends[d], "x", d) for d in (1, 2, 3)]
    own, ahead_one, far, behind_one = down(pieces, down_all, x)
    via_ahead, via_behind = shift(far[:48], "y", 1), shift(far[48:], "y", -1)

    ahead_one = jnp.concatenate([added(ahead_one[:48], via_ahead), ahead_one[48:]], axis=0)
    behind_one = jnp.concatenate([behind_one[:48], added(behind_one[48:], via_behind)], axis=0)
    parts = [own, shift(ahead_one, "y", 1), shift(behind_one, "y", -1)]
    own1, own2, own3, stayed, crossing, opposite = refold(parts, unfold.transpose(0, 2, 1))
    crossing = swap(crossing, "c")
    home = [
        part_ways(jnp.concatenate([own, crossing[48 * j : 48 * j + 48]], axis=0), j + 1, True)
        for j, own in enumerate((own1, own2, own3))
    ]
    opposite = part_ways(opposite, 4, True)
    kept = [v[at : at + 24] for v in home for at in (0, 48)] + [opposite[:24], stayed[:24]]
    given = [v[at : at + 24] for v in home for at in (24, 72)] + [opposite[24:], stayed[24:]]
    kept = jnp.concatenate(kept, axis=0)
    given = swap(jnp.concatenate(given, axis=0), "c")

    gates_rel = gates.reshape(TOK, NC, NZ).transpose(1, 2, 0)
    spread = jnp.broadcast_to(
        gates_rel[:, :, None, None, None, :], (NC, NZ, QUARTERS, CAP, QUARTERS, TOK)
    ).reshape(NC, NZ * QUARTERS * CAP, QUARTERS * TOK)
    weights = jnp.where(dispatch, spread, 0.0)
    combined = 0.0
    for rows, weight in ((kept, weights[0]), (given, weights[1])):
        for part in split_hi_lo(weight):
            combined = combined + lax.dot_general(
                part, rows, (((0,), (0,)), ((), ())), preferred_element_type=F32
            )
    combined = jnp.concatenate(
        [combined[i * TOK : (i + 1) * TOK] for i in range(QUARTERS)], axis=1
    )
    return (hidden + combined).astype(BF16)


def solution(mesh):
    grid = Mesh(mesh.devices.reshape(NX, NY, NZ, NC), ("x", "y", "z", "c"))
    seq, exp = ("x", "y"), ("z", "c")
    placed = (
        P(seq, exp),
        P(seq, exp),
        P(seq, exp),
        P(seq, exp),
        P(seq + exp, None),
        P(exp, None),
        P(),
        P(exp, None, seq),
        P(exp, None, seq),
        P(exp, seq, None),
        P(seq + exp, None),
    )
    return jax.shard_map(
        shards, mesh=grid, in_specs=placed, out_specs=P(seq + exp, None), check_vma=False
    )
```

```python
import jax
import jax.numpy as jnp
from jax import lax
from jax.experimental import pallas as pl
from jax.experimental.pallas import tpu as pltpu
from jax.sharding import Mesh, PartitionSpec as P

D = 3072
HEAD_DIM = 128
TOK = 32
CAP = 6
QUARTERS = 4
QCOLS = D // QUARTERS
NX, NY, NZ, NC = 4, 4, 8, 2
SIZES = {"x": NX, "y": NY, "z": NZ, "c": NC}
F32, BF16 = jnp.float32, jnp.bfloat16


def shift(v, axis, by):
    n = SIZES[axis]
    return lax.ppermute(v, axis, [(i, (i + by) % n) for i in range(n)])


def part_ways(v, by, back=False):
    pairs = []
    for z in range(NZ):
        for c in range(NC):
            there = (z + (1 - 2 * c) * by) % NZ
            pairs.append((z * NC + c, there * NC + c))
    if back:
        pairs = [(there, here) for here, there in pairs]
    return lax.ppermute(v, ("z", "c"), pairs)


def swap(v, axis):
    return lax.ppermute(v, axis, [(i, i ^ 1) for i in range(SIZES[axis])])


def ahead(v, axis):
    return [v, shift(v, axis, -1), shift(v, axis, 2), shift(v, axis, 1)]


def ahead_split(v, axis):
    up, down = shift(v, axis, -1), shift(v, axis, 1)
    half = v.shape[0] // 2
    far = jnp.concatenate([shift(up[:half], axis, -1), shift(down[half:], axis, 1)], axis=0)
    return [v, up, far, down]


def dot(a, b):
    return jnp.dot(a, b, preferred_element_type=F32)


def added(a, b):
    return (a.astype(F32) + b.astype(F32)).astype(BF16)


def split_hi_lo(v):
    hi = v.astype(BF16)
    return hi, (v - hi.astype(F32)).astype(BF16)


MSG = HEAD_DIM + 16


def parts_of(v):
    hi, rest = split_hi_lo(v)
    mid = (v - hi.astype(F32)).astype(BF16)
    return hi, mid, (v - hi.astype(F32) - mid.astype(F32)).astype(BF16)


def message_rows(total):
    hi, lo = split_hi_lo(total)
    row = lax.broadcasted_iota(jnp.int32, (16, HEAD_DIM), 0)
    rows = jnp.where(row == 0, hi.astype(F32), jnp.where(row == 1, lo.astype(F32), 0.0))
    return rows.astype(BF16)


def state_kernel(k_ref, v_ref, decay_ref, message_ref, col_ref, row_ref):
    rows = k_ref.shape[0]
    lane = lax.broadcasted_iota(jnp.int32, (rows, HEAD_DIM), 1)
    decay = jnp.where(lane < 64, decay_ref[:, 0:1], decay_ref[:, 1:2])
    tri = (
        lax.broadcasted_iota(jnp.int32, (rows, rows), 0)
        >= lax.broadcasted_iota(jnp.int32, (rows, rows), 1)
    ).astype(F32).astype(BF16)
    col, row = 0.0, 0.0
    for part in parts_of(decay):
        col = col + dot(tri, part)
        row = row + lax.dot_general(
            part, tri, (((0,), (1,)), ((), ())), preferred_element_type=F32
        )
    col_ref[...] = col
    for h in range(2):
        row_ref[h * 8 : h * 8 + 8] = row[h * 64 : h * 64 + 8]
        cols = slice(h * HEAD_DIM, (h + 1) * HEAD_DIM)
        here = jnp.broadcast_to(col[:, h * 64 : h * 64 + 1], (rows, HEAD_DIM))
        tail = here[rows - 1 : rows]
        scaled = k_ref[:, cols].astype(F32) * jnp.exp(tail - here)
        state = 0.0
        for part in split_hi_lo(scaled):
            state = state + lax.dot_general(
                part, v_ref[:, cols], (((0,), (0,)), ((), ())), preferred_element_type=F32
            )
        message_ref[h, :HEAD_DIM] = state.astype(BF16)
        message_ref[h, HEAD_DIM:] = message_rows(tail)


def within_kernel(q_ref, k_ref, v_ref, col_ref, row_ref, out_ref):
    rows = q_ref.shape[0]
    step = 256
    for h in range(2):
        cols = slice(h * HEAD_DIM, (h + 1) * HEAD_DIM)
        for start in range(0, rows, step):
            stop = start + step
            scores = lax.dot_general(
                q_ref[start:stop, cols],
                k_ref[:stop, cols],
                (((1,), (1,)), ((), ())),
                preferred_element_type=F32,
            )
            apart = col_ref[start:stop, h * 64 : h * 64 + 1] - row_ref[h * 8 : h * 8 + 1, :stop]
            causal = start + lax.broadcasted_iota(
                jnp.int32, (step, stop), 0
            ) >= lax.broadcasted_iota(jnp.int32, (step, stop), 1)
            damped = scores * jnp.where(causal, jnp.exp(jnp.minimum(apart, 0.0)), 0.0)
            total = 0.0
            for part in split_hi_lo(damped):
                total = total + dot(part, v_ref[:stop, cols])
            out_ref[start:stop, cols] = total


def fold(messages, h, place):
    totals = [m[h, HEAD_DIM:].astype(F32) for m in messages]
    totals = [t[0:1] + t[1:2] for t in totals]
    states = [m[h, :HEAD_DIM].astype(F32) for m in messages]
    where = [lax.rem(place + 4 - d, 4) for d in range(4)]
    ordered = [sum(jnp.where(where[d] == j, totals[d], 0.0) for d in range(4)) for j in range(4)]
    before, everything = 0.0, 0.0
    for d in range(4):
        till_here = sum(
            jnp.where((j > where[d]) & (j < place), ordered[j], 0.0) for j in range(4)
        )
        till_end = sum(jnp.where(j > where[d], ordered[j], 0.0) for j in range(4))
        before = before + jnp.where(where[d] < place, jnp.exp(till_here), 0.0) * states[d]
        everything = everything + jnp.exp(till_end) * states[d]
    total_before = sum(jnp.where(j < place, ordered[j], 0.0) for j in range(4))
    return before, total_before, everything, sum(ordered)


def fold_kernel(place_ref, m0, m1, m2, m3, message_ref, before_ref):
    for h in range(2):
        before, total_before, everything, total = fold((m0, m1, m2, m3), h, place_ref[0])
        before_ref[h, :HEAD_DIM] = before
        before_ref[h, HEAD_DIM:] = jnp.broadcast_to(jnp.exp(total_before), (8, HEAD_DIM))
        message_ref[h, :HEAD_DIM] = everything.astype(BF16)
        message_ref[h, HEAD_DIM:] = message_rows(total)


def mix_kernel(
    place_ref, m0, m1, m2, m3, before_ref, q_ref, col_ref, within_ref, mine_ref, other_ref, held
):
    for h in range(2):
        cols = slice(h * HEAD_DIM, (h + 1) * HEAD_DIM)
        earlier, _, _, _ = fold((m0, m1, m2, m3), h, place_ref[0])
        state = before_ref[h, :HEAD_DIM] + before_ref[h, HEAD_DIM : HEAD_DIM + 1] * earlier
        carried = 0.0
        for part in split_hi_lo(state):
            carried = carried + dot(q_ref[:, cols], part)
        mixed = within_ref[:, cols] + jnp.exp(col_ref[:, h * 64 : h * 64 + 1]) * carried
        scale = lax.rsqrt(jnp.mean(mixed * mixed, axis=-1, keepdims=True) + 1e-06)
        held[:, cols] = (mixed * scale).astype(BF16)
    core = place_ref[1]
    for i in range(NZ):
        at = pl.multiple_of(i * 2 * TOK + core * TOK, TOK)
        mine_ref[i * TOK : (i + 1) * TOK] = held[pl.ds(at, TOK)]
        at = pl.multiple_of(i * 2 * TOK + (1 - core) * TOK, TOK)
        other_ref[i * TOK : (i + 1) * TOK] = held[pl.ds(at, TOK)]


def local_kernel(body, outs, scalars=(), scratch=(), flops=1 << 27, grant=16):
    vmem = pl.BlockSpec(memory_space=pltpu.VMEM)
    smem = pl.BlockSpec(memory_space=pltpu.SMEM)

    def call(*operands):
        given = (jnp.stack([s.astype(jnp.int32) for s in scalars]),) if scalars else ()
        return pl.pallas_call(
            body,
            out_shape=[jax.ShapeDtypeStruct(*o) for o in outs],
            in_specs=[smem] * len(given) + [vmem] * len(operands),
            out_specs=[vmem] * len(outs),
            scratch_shapes=list(scratch),
            compiler_params=pltpu.CompilerParams(vmem_limit_bytes=grant << 20),
            cost_estimate=pl.CostEstimate(
                flops=flops, bytes_accessed=2 << 20, transcendentals=1 << 18
            ),
        )(*given, *operands)

    return call


def state_call(keys, values, log_decay):
    rows = keys.shape[0]
    return local_kernel(
        state_kernel,
        [((2, MSG, HEAD_DIM), BF16), ((rows, HEAD_DIM), F32), ((16, rows), F32)],
        flops=1 << 28,
    )(keys, values, log_decay)


def within_call(queries, keys, values, col, row):
    return local_kernel(within_kernel, [(queries.shape, F32)], flops=1 << 29)(
        queries, keys, values, col, row
    )[0]


def fold_call(messages, place):
    return local_kernel(
        fold_kernel,
        [((2, MSG, HEAD_DIM), BF16), ((2, HEAD_DIM + 8, HEAD_DIM), F32)],
        scalars=(place,),
    )(*messages)


def mix_call(messages, before, queries, col, within, place, core):
    rows, cols = queries.shape
    return local_kernel(
        mix_kernel,
        [((rows // 2, cols), BF16)] * 2,
        scalars=(place, core),
        scratch=[pltpu.VMEM((rows, cols), BF16)],
    )(*messages, before, queries, col, within)


def attention(queries, keys, values, log_decay):
    message, col, row = state_call(keys, values, log_decay)
    messages = [message] + [shift(message, "y", d) for d in (1, 2, 3)]
    within = within_call(queries, keys, values, col, row)
    message, before = fold_call(messages, lax.axis_index("y"))
    messages = [message] + [shift(message, "x", d) for d in (1, 2, 3)]
    places = [lax.axis_index(a) for a in ("x", "c")]
    return mix_call(messages, before, queries, col, within, *places)


def arrange_kernel(a_ref, b_ref, c_ref, *outs):
    first = [(a_ref, 0), (b_ref, 0), (c_ref, 0), (b_ref, 1)]
    second = [(a_ref, 1), (b_ref, 2), (c_ref, 1), (b_ref, 3)]
    for dx in range(4):
        for dy in range(4):
            ref, at = first[dy]
            outs[dx][dy * 96 : dy * 96 + 48] = ref[at * 192 + dx * 48 : at * 192 + dx * 48 + 48]
            ref, at = second[dx]
            outs[dx][dy * 96 + 48 : dy * 96 + 96] = ref[
                at * 192 + dy * 48 : at * 192 + dy * 48 + 48
            ]


def arrange(a, b, c):
    units = a.shape[1]
    return pl.pallas_call(
        arrange_kernel,
        out_shape=[jax.ShapeDtypeStruct((384, units), BF16)] * 4,
        compiler_params=pltpu.CompilerParams(vmem_limit_bytes=6 << 20),
        cost_estimate=pl.CostEstimate(flops=0, bytes_accessed=2 << 20, transcendentals=0),
    )(a, b, c)


def beside_kernel(place_ref, p0, p1, p2, p3, out_ref):
    units = p0.shape[1]
    for d, piece in enumerate((p0, p1, p2, p3)):
        at = lax.rem(place_ref[0] + 4 - d, 4)
        out_ref[:, pl.ds(pl.multiple_of(at * units, 128), units)] = piece[...]


def down(pieces, weights, place):
    rows, units = pieces[0].shape
    beside = local_kernel(
        beside_kernel, [((rows, 4 * units), BF16)], scalars=(place,), flops=1 << 20, grant=6
    )(*pieces)[0]
    leaving = dot(beside[96:], weights).astype(BF16)
    own = dot(beside[:96], weights).astype(BF16)
    return [own] + [leaving[i * 96 : i * 96 + 96] for i in range(3)]


def refold_kernel(p0, p1, p2, fold_ref, *outs):
    for half in range(2):
        at = slice(half * 48, half * 48 + 48)
        total = sum(p[at].astype(F32) for p in (p0, p1, p2)).astype(BF16)
        rows = 0.0
        for i in range(QUARTERS):
            rows = rows + dot(fold_ref[i], total[:, i * QCOLS : (i + 1) * QCOLS])
        rows = rows.astype(BF16)
        row = 0
        for out in outs[:4] if half == 0 else outs[4:]:
            out[...] = rows[row : row + out.shape[0]]
            row += out.shape[0]


def refold(parts, fold):
    return pl.pallas_call(
        refold_kernel,
        out_shape=[jax.ShapeDtypeStruct((n, QCOLS), BF16) for n in (48, 48, 48, 48, 144, 48)],
        compiler_params=pltpu.CompilerParams(vmem_limit_bytes=12 << 20),
        cost_estimate=pl.CostEstimate(flops=2 << 27, bytes_accessed=3 << 20, transcendentals=0),
    )(*parts, fold)


def unfold_matrix():
    row = jnp.arange(48)
    place, core, slot = row // 12, (row // 6) % 2, row % 6
    quarter = jnp.arange(QUARTERS)[:, None]
    source = place * 48 + core * 24 + quarter * 6 + slot
    return (source[:, :, None] == jnp.arange(192)[None, None, :]).astype(BF16)


def shards(
    queries, keys, values, log_decay, residual, out_weight, router, w_gate, w_up, w_down, routes
):
    z, c = lax.axis_index("z"), lax.axis_index("c")
    x = lax.axis_index("x")
    down_all = lax.all_gather(w_down[0], "x", axis=0, tiled=True)
    weight_pair = jnp.concatenate([out_weight, swap(out_weight, "c")], axis=0)
    gate_up = jnp.concatenate([w_gate[0], w_up[0]], axis=1)

    ids = jnp.arange(16)
    carrier = c ^ (ids // 8)
    kind = ids % 8
    away = jnp.where(kind < 6, (1 - 2 * carrier) * (kind // 2 + 1), jnp.where(kind == 6, 4, 0))
    crossed = jnp.where(kind < 6, kind % 2, 0)
    relative = 2 * ((z + away + NZ) % NZ) + (carrier ^ crossed)
    named = (routes[:, :, None] == relative[None, None, :]).any(axis=1)
    member = named.astype(F32)
    earlier = (jnp.arange(TOK)[:, None] > jnp.arange(TOK)[None, :]).astype(F32)
    slot = jnp.dot(earlier, member).astype(jnp.int32)
    router_rel = dot(
        router, (ids[:, None] == relative[None, :]).astype(BF16)
    ).astype(BF16)
    chosen = named[:, :, None] & (slot[:, :, None] == jnp.arange(CAP)[None, None, :])
    chosen = chosen.reshape(TOK, NC, NZ, CAP).transpose(1, 2, 3, 0)
    same = jnp.eye(QUARTERS, dtype=jnp.bool_)
    dispatch = chosen[:, :, None, :, None, :] & same[None, None, :, None, :, None]
    dispatch = dispatch.reshape(NC, NZ * QUARTERS * CAP, QUARTERS * TOK)
    dispatch_bf = dispatch.astype(BF16)

    mine, theirs = attention(queries, keys, values, log_decay)
    both = jnp.concatenate([mine, swap(theirs, "c")], axis=1)
    projected = dot(both, weight_pair).astype(BF16).reshape(NZ, TOK, D)

    def block(d):
        return lax.dynamic_index_in_dim(projected, (z + d) % NZ, 0, keepdims=False)

    half = TOK // 2
    from_below = shift(jnp.concatenate([block(2), block(4)[:half]], axis=0), "z", 1)
    from_above = shift(jnp.concatenate([block(6), block(4)[half:]], axis=0), "z", -1)
    three_up, three_down = block(3), block(5)
    sums = [
        (3, jnp.concatenate([added(three_up[:half], from_below[TOK:]), three_up[half:]], axis=0)),
        (5, jnp.concatenate([three_down[:half], added(three_down[half:], from_above[TOK:])], axis=0)),
        (1, added(block(1), from_below[:TOK])),
        (7, added(block(7), from_above[:TOK])),
    ]
    attn = block(0).astype(F32)
    for d, total in sums:
        attn = attn + shift(total, "z", d).astype(F32)
    hidden = residual.astype(F32) + attn
    normed = (hidden * lax.rsqrt(jnp.mean(hidden * hidden, axis=-1, keepdims=True) + 1e-06)).astype(
        BF16
    )
    logits = dot(normed, router_rel)
    picked = jax.nn.sigmoid(logits) * member
    gates = picked / jnp.sum(picked, axis=1, keepdims=True)

    folded = jnp.concatenate(
        [normed[:, i * QCOLS : (i + 1) * QCOLS] for i in range(QUARTERS)], axis=0
    )
    keep = dot(dispatch_bf[0], folded).astype(BF16).reshape(8, 24, QCOLS)
    got = swap(dot(dispatch_bf[1], folded).astype(BF16), "c").reshape(8, 24, QCOLS)
    out_rows = [
        jnp.concatenate([keep[2 * j], got[2 * j], keep[2 * j + 1], got[2 * j + 1]], axis=0)
        for j in range(3)
    ]
    opposite = jnp.concatenate([keep[6], got[6]], axis=0)
    stayed = jnp.concatenate([keep[7], got[7]], axis=0)
    opposite = part_ways(opposite, 4)
    arrived = [part_ways(out_rows[j], j + 1) for j in range(3)]
    opposite, *arrived = lax.optimization_barrier((opposite, *arrived))
    crossing = swap(jnp.concatenate([v[48:] for v in arrived], axis=0), "c")
    unfold = unfold_matrix()

    def unfolded(blocks):
        block = jnp.concatenate(blocks, axis=0)
        return jnp.concatenate(
            [dot(unfold[i], block).astype(BF16) for i in range(QUARTERS)], axis=1
        )

    first = unfolded([v[:48] for v in arrived] + [stayed])
    second = unfolded([crossing, opposite])
    rows_x, rows_y = lax.optimization_barrier(
        (
            jnp.concatenate(ahead(first, "x"), axis=0),
            jnp.concatenate(ahead(second, "y"), axis=0),
        )
    )
    by_y, by_x = ahead_split(rows_x, "y"), ahead_split(rows_y, "x")
    by_y[1], down_all = lax.optimization_barrier((by_y[1], down_all))

    def expert_hidden(blocks):
        product = dot(jnp.concatenate(blocks, axis=0), gate_up)
        gate_part, up_part = jnp.split(product, 2, axis=1)
        return (jax.nn.silu(gate_part) * up_part).astype(BF16)

    hidden_a = expert_hidden([by_y[0], by_x[0]])
    hidden_b = expert_hidden([by_y[1], by_y[3], by_x[1], by_x[3]])
    hidden_c = expert_hidden([by_y[2], by_x[2]])
    sends = arrange(hidden_a, hidden_b, hidden_c)
    pieces = [sends[0]] + [shift(sends[d], "x", d) for d in (1, 2, 3)]
    own, ahead_one, far, behind_one = down(pieces, down_all, x)
    via_ahead, via_behind = shift(far[:48], "y", 1), shift(far[48:], "y", -1)

    ahead_one = jnp.concatenate([added(ahead_one[:48], via_ahead), ahead_one[48:]], axis=0)
    behind_one = jnp.concatenate([behind_one[:48], added(behind_one[48:], via_behind)], axis=0)
    parts = [own, shift(ahead_one, "y", 1), shift(behind_one, "y", -1)]
    own1, own2, own3, stayed, crossing, opposite = refold(parts, unfold.transpose(0, 2, 1))
    crossing = swap(crossing, "c")
    home = [
        part_ways(jnp.concatenate([own, crossing[48 * j : 48 * j + 48]], axis=0), j + 1, True)
        for j, own in enumerate((own1, own2, own3))
    ]
    opposite = part_ways(opposite, 4, True)
    kept = [v[at : at + 24] for v in home for at in (0, 48)] + [opposite[:24], stayed[:24]]
    given = [v[at : at + 24] for v in home for at in (24, 72)] + [opposite[24:], stayed[24:]]
    kept = jnp.concatenate(kept, axis=0)
    given = swap(jnp.concatenate(given, axis=0), "c")

    gates_rel = gates.reshape(TOK, NC, NZ).transpose(1, 2, 0)
    spread = jnp.broadcast_to(
        gates_rel[:, :, None, None, None, :], (NC, NZ, QUARTERS, CAP, QUARTERS, TOK)
    ).reshape(NC, NZ * QUARTERS * CAP, QUARTERS * TOK)
    weights = jnp.where(dispatch, spread, 0.0)
    combined = 0.0
    for rows, weight in ((kept, weights[0]), (given, weights[1])):
        for part in split_hi_lo(weight):
            combined = combined + lax.dot_general(
                part, rows, (((0,), (0,)), ((), ())), preferred_element_type=F32
            )
    combined = jnp.concatenate(
        [combined[i * TOK : (i + 1) * TOK] for i in range(QUARTERS)], axis=1
    )
    return (hidden + combined).astype(BF16)


def solution(mesh):
    grid = Mesh(mesh.devices.reshape(NX, NY, NZ, NC), ("x", "y", "z", "c"))
    seq, exp = ("x", "y"), ("z", "c")
    placed = (
        P(seq, exp),
        P(seq, exp),
        P(seq, exp),
        P(seq, exp),
        P(seq + exp, None),
        P(exp, None),
        P(),
        P(exp, None, seq),
        P(exp, None, seq),
        P(exp, seq, None),
        P(seq + exp, None),
    )
    return jax.shard_map(
        shards, mesh=grid, in_specs=placed, out_specs=P(seq + exp, None), check_vma=False
    )
```
